32 devices in a mesh: rows: 32 (over z, y, x, core).
Axes of the slice: x: 2, y: 2, z: 4, core: 2. Of those that a mesh axis runs over, the one named last changes fastest.
Arguments:
- bases: float32 [5, 32768, 128], P(None, 'rows'), may hold values from -1 to 1
- targets: float32 [32768, 128], P('rows'), may hold values from -8 to 8
Outputs:
- solved: float32 [32768, 128], P('rows')
The draws below stay inside these ranges and needn't reach their ends.
All inputs are finite; a program needn't handle non-finite values.
Results may differ from the reference program's by a relative error of at most 0.0001.
Values sent between devices are 32-bit elements; how exact they have to be, the bound alone decides.
A program may use at most 64 MiB of HBM per device.

```python
import jax
import jax.numpy as jnp
from jax import lax

K = 128
LEVELS = 5
N = 32768


def noise_field(sub_key, shape):
    return jnp.clip(jax.random.normal(sub_key, shape, jnp.float32), -4.0, 4.0)


def build_fields(key):
    scales = [(0.2 * 2 ** (level_no + 1) / N) ** 0.5 for level_no in range(LEVELS)]
    raw_fields = [noise_field(jax.random.fold_in(key, 100 + level_no), (N, K)) * scales[level_no] for level_no in range(LEVELS)]
    made_bases = []
    for coarse_no in range(LEVELS):
        field = raw_fields[coarse_no]
        for fine_no in range(coarse_no + 1, LEVELS):
            blocks = 2 ** (fine_no + 1)
            factor = (0.1 * scales[coarse_no] ** 2 / (scales[fine_no] ** 2 * K)) ** 0.5
            mixing = noise_field(jax.random.fold_in(key, 200 + 10 * coarse_no + fine_no), (blocks, K, K)) * factor
            nested = jnp.einsum('crk,ckl->crl', raw_fields[fine_no].reshape(blocks, N // blocks, K), mixing, precision=lax.Precision.HIGHEST)
            field = field + nested.reshape(N, K)
        made_bases.append(jnp.clip(field, -1.0, 1.0))
    made_targets = noise_field(jax.random.fold_in(key, 300), (N, K)) * (1.0 / (LEVELS + 1)) ** 0.5
    for fine_no in range(LEVELS):
        blocks = 2 ** (fine_no + 1)
        factor = (1.0 / ((LEVELS + 1) * K * scales[fine_no] ** 2)) ** 0.5
        mixing = noise_field(jax.random.fold_in(key, 400 + fine_no), (blocks, K, K)) * factor
        nested = jnp.einsum('crk,ckl->crl', raw_fields[fine_no].reshape(blocks, N // blocks, K), mixing, precision=lax.Precision.HIGHEST)
        made_targets = made_targets + nested.reshape(N, K)
    return (jnp.stack(made_bases), jnp.clip(made_targets, -8.0, 8.0))


def draw_bases(key, part):
    return build_fields(key)[0]


def draw_targets(key, part):
    return build_fields(key)[1]


def setup_inputs(seed: int = 0) -> dict:
    streams_of = jax.random.split(jax.random.key(seed), 3)
    return {
        "bases": draw_bases(jax.random.fold_in(streams_of[2], 71), 0),
        "targets": draw_targets(jax.random.fold_in(streams_of[2], 71), 0),
    }


def solve_core(left_sums, right_sums):
    identity = jnp.eye(left_sums.shape[-1], dtype=jnp.float32)
    gram_a = left_sums[0]
    gram_b = right_sums[0]
    proj_a = left_sums[1:]
    proj_b = right_sums[1:]
    chol_a = jnp.linalg.cholesky(gram_a)
    inverse_a = jax.scipy.linalg.cho_solve((chol_a, True), identity)
    schur_part = inverse_a - gram_b
    chol_s = jnp.linalg.cholesky(schur_part)
    inverse_s = jax.scipy.linalg.cho_solve((chol_s, True), identity)
    target_b = jnp.einsum('kl,mln->mkn', inverse_a, proj_a, precision=lax.Precision.HIGHEST) - proj_b
    coef_b = jnp.einsum('kl,mln->mkn', inverse_s, target_b, precision=lax.Precision.HIGHEST)
    coef_a = proj_b - jnp.einsum('kl,mln->mkn', gram_b, coef_b, precision=lax.Precision.HIGHEST)
    return (coef_a, coef_b)

def reference(bases, targets):
    n_total = bases.shape[1]
    rank = bases.shape[2]
    fields = [bases[level_no] for level_no in range(LEVELS)] + [targets]
    for level_no in reversed(range(LEVELS)):
        blocks = 2 ** (level_no + 1)
        rows_child = n_total // blocks
        own_basis = fields[level_no].reshape(blocks, rows_child, rank)
        coarser = jnp.stack(fields[:level_no] + [fields[LEVELS]]).reshape(level_no + 1, blocks, rows_child, rank)
        gram = jnp.einsum('crk,crl->ckl', own_basis, own_basis, precision=lax.Precision.HIGHEST)
        proj = jnp.einsum('crk,mcrl->cmkl', own_basis, coarser, precision=lax.Precision.HIGHEST)
        payload = jnp.concatenate([gram[:, None], proj], 1)
        coef_a, coef_b = jax.vmap(solve_core)(payload[0::2], payload[1::2])
        coefs = jnp.stack([coef_a, coef_b], 1).reshape(blocks, level_no + 1, rank, rank)
        corrected = coarser - jnp.einsum('crk,cmkl->mcrl', own_basis, coefs, precision=lax.Precision.HIGHEST)
        corrected = corrected.reshape(level_no + 1, n_total, rank)
        fields = [corrected[m_no] for m_no in range(level_no)] + fields[level_no:LEVELS] + [corrected[level_no]]
    return fields[LEVELS]
```

```python
import functools

import jax
import jax.numpy as jnp
from jax import lax
from jax.experimental import pallas as pl
from jax.experimental.pallas import tpu as pltpu
from jax.sharding import PartitionSpec as P

AXIS = "rows"
VMEM_LIMIT = 48 * 2**20
VMEM_SPEC = pl.BlockSpec(memory_space=pltpu.VMEM)


def offset(level_no):
    return level_no * (level_no + 3) // 2


def split(value):
    high = value.astype(jnp.bfloat16)
    low = (value - high.astype(jnp.float32)).astype(jnp.bfloat16)
    return high, low


def dot_split(left, right):
    left_high, left_low = left
    right_high, right_low = right
    dot = functools.partial(jnp.dot, preferred_element_type=jnp.float32)
    return (dot(left_low, right_high) + dot(left_high, right_low)) + dot(left_high, right_high)


def dot3(left, right):
    return dot_split(split(left), split(right))


def wide(blocks):
    return jnp.concatenate(blocks, axis=1)


def gram_rows(bases_ref, targets_ref, store):
    levels = bases_ref.shape[0]
    rank = bases_ref.shape[2]
    parts = [split(targets_ref[...])]
    for level_no in range(levels):
        basis = bases_ref[level_no]
        parts.append(split(basis))
        turned = split(basis.T)
        rhs = (wide([part[0] for part in parts]), wide([part[1] for part in parts]))
        row = dot_split(turned, rhs)
        for col in range(level_no + 2):
            store(offset(level_no) + col, row[:, col * rank : (col + 1) * rank])


def eye(rank):
    shape = (rank, rank)
    row = lax.broadcasted_iota(jnp.int32, shape, 0)
    col = lax.broadcasted_iota(jnp.int32, shape, 1)
    return (row == col).astype(jnp.float32)


def square_step(inverse, power):
    rank = power.shape[0]
    both = dot3(power, wide([inverse, power]))
    return inverse + both[:, :rank], both[:, rank:]


def solve_pair(left_row, right_row, inverse_of):
    rank = left_row.shape[0]
    gram_a, gram_b = left_row[:, -rank:], right_row[:, -rank:]
    proj_a, proj_b = left_row[:, :-rank], right_row[:, :-rank]
    first = dot3(gram_a, wide([gram_b, proj_b]))
    inverse = inverse_of(first[:, :rank])
    coef_b = dot3(inverse, proj_a - first[:, rank:])
    coef_a = proj_b - dot3(gram_b, coef_b)
    return coef_a, coef_b


def adaptive_inverse(matrix):
    identity = eye(matrix.shape[0])

    def unfinished(state):
        step, _, power = state
        size = jnp.sum(power * power)
        return jnp.logical_and(size > 1e-14, step < 64)

    def body(state):
        step, inverse, power = state
        inverse, power = square_step(inverse, power)
        return step + 1, inverse, power

    state = (0, identity + matrix, dot3(matrix, matrix))
    return lax.while_loop(unfinished, body, state)[1]


def merged_rows(level_no, own, sib, sides, coef_a, coef_b, store):
    rank = coef_a.shape[0]
    proj_a, proj_b = sides[0][:, :-rank], sides[1][:, :-rank]
    stacked = jnp.concatenate([coef_a, coef_b], axis=0)
    rhs = split(jnp.concatenate([proj_a + coef_b, proj_b + coef_a], axis=0))
    for row_no in range(level_no):
        columns = slice((row_no + 1) * rank, (row_no + 2) * rank)
        turned = split(stacked[:, columns].T)
        end = (row_no + 2) * rank
        change = dot_split(turned, (rhs[0][:, :end], rhs[1][:, :end]))
        for col in range(row_no + 2):
            slot = offset(row_no) + col
            store(slot, own(slot) + sib(slot) - change[:, col * rank : (col + 1) * rank])


def final_coefs(coef_of, levels):
    deltas = []
    for level_no in range(levels):
        delta = coef_of(level_no, 0)
        if deltas:
            known = jnp.concatenate(deltas, axis=0)
            delta = delta - dot3(wide([coef_of(level_no, 1 + i) for i in range(level_no)]), known)
        deltas.append(delta)
    return deltas


def gram_kernel(bases_ref, targets_ref, out_ref):
    def store(slot, value):
        out_ref[slot] = value

    gram_rows(bases_ref, targets_ref, store)


def level_kernel(level_no, group_bits, own_ref, sib_ref, *out_refs):
    coef_ref = out_refs[0]
    is_left = lax.rem(lax.axis_index(AXIS) // 2**group_bits, 2) == 0
    base = offset(level_no)
    own_row = wide([own_ref[base + col] for col in range(level_no + 2)])
    sib_row = wide([sib_ref[base + col] for col in range(level_no + 2)])
    sides = (jnp.where(is_left, own_row, sib_row), jnp.where(is_left, sib_row, own_row))
    coef_a, coef_b = solve_pair(*sides, adaptive_inverse)
    own_coef = jnp.where(is_left, coef_a, coef_b)
    rank = coef_a.shape[0]
    for col in range(level_no + 1):
        coef_ref[col] = own_coef[:, col * rank : (col + 1) * rank]
    if level_no:
        next_ref = out_refs[1]

        def store(slot, value):
            next_ref[slot] = value

        merged_rows(
            level_no, lambda s: own_ref[s], lambda s: sib_ref[s], sides, coef_a, coef_b, store
        )


def apply_kernel(bases_ref, targets_ref, *refs):
    levels = bases_ref.shape[0]
    coefs, out_ref = refs[:-1], refs[-1]
    deltas = final_coefs(lambda level_no, col: coefs[level_no][col], levels)
    lhs = wide([bases_ref[level_no] for level_no in range(levels)])
    out_ref[...] = targets_ref[...] - dot3(lhs, jnp.concatenate(deltas, axis=0))


def call(kernel, outs, args):
    return pl.pallas_call(
        kernel,
        out_shape=outs,
        in_specs=[VMEM_SPEC] * len(args),
        out_specs=jax.tree.map(lambda _: VMEM_SPEC, outs),
        compiler_params=pltpu.CompilerParams(vmem_limit_bytes=VMEM_LIMIT),
    )(*args)


def from_partner(value, bit_no):
    pairs = [(source, source ^ 2**bit_no) for source in range(lax.axis_size(AXIS))]
    return lax.ppermute(value, AXIS, pairs)


def blocks(count, rank):
    return jax.ShapeDtypeStruct((count, rank, rank), jnp.float32)


def per_device(bases, targets):
    levels, _, rank = bases.shape
    tree_depth = lax.axis_size(AXIS).bit_length() - 1
    sums = call(gram_kernel, blocks(offset(levels), rank), (bases, targets))
    for bit_no in range(tree_depth - levels):
        sums = sums + from_partner(sums, bit_no)
    coefs = [None] * levels
    for level_no in reversed(range(levels)):
        group_bits = tree_depth - level_no - 1
        sibling = from_partner(sums, group_bits)
        outs = [blocks(level_no + 1, rank)]
        if level_no:
            outs.append(blocks(offset(level_no), rank))
        kernel = functools.partial(level_kernel, level_no, group_bits)
        coefs[level_no], *rest = call(kernel, tuple(outs), (sums, sibling))
        sums = rest[0] if rest else None
    out = jax.ShapeDtypeStruct(targets.shape, jnp.float32)
    return call(apply_kernel, out, (bases, targets, *coefs))


def solution(mesh):
    return jax.shard_map(
        per_device,
        mesh=mesh,
        in_specs=(P(None, AXIS, None), P(AXIS, None)),
        out_specs=P(AXIS, None),
        check_vma=False,
    )
```

```python
import functools

import jax
import jax.numpy as jnp
from jax import lax
from jax.experimental import pallas as pl
from jax.experimental.pallas import tpu as pltpu
from jax.sharding import PartitionSpec as P

AXIS = "rows"
VMEM_LIMIT = 48 * 2**20
VMEM_SPEC = pl.BlockSpec(memory_space=pltpu.VMEM)


def offset(level_no):
    return level_no * (level_no + 3) // 2


def split(value):
    high = value.astype(jnp.bfloat16)
    low = (value - high.astype(jnp.float32)).astype(jnp.bfloat16)
    return high, low


def dot_split(left, right):
    left_high, left_low = left
    right_high, right_low = right
    dot = functools.partial(jnp.dot, preferred_element_type=jnp.float32)
    return (dot(left_low, right_high) + dot(left_high, right_low)) + dot(left_high, right_high)


def dot3(left, right):
    return dot_split(split(left), split(right))


def wide(blocks):
    return jnp.concatenate(blocks, axis=1)


def gram_rows(bases_ref, targets_ref, store):
    levels = bases_ref.shape[0]
    rank = bases_ref.shape[2]
    parts = [split(targets_ref[...])]
    for level_no in range(levels):
        basis = bases_ref[level_no]
        parts.append(split(basis))
        turned = split(basis.T)
        rhs = (wide([part[0] for part in parts]), wide([part[1] for part in parts]))
        row = dot_split(turned, rhs)
        for col in range(level_no + 2):
            store(offset(level_no) + col, row[:, col * rank : (col + 1) * rank])


def eye(rank):
    shape = (rank, rank)
    row = lax.broadcasted_iota(jnp.int32, shape, 0)
    col = lax.broadcasted_iota(jnp.int32, shape, 1)
    return (row == col).astype(jnp.float32)


def square_step(inverse, power):
    rank = power.shape[0]
    both = dot3(power, wide([inverse, power]))
    return inverse + both[:, :rank], both[:, rank:]


def solve_pair(left_row, right_row, inverse_of):
    rank = left_row.shape[0]
    gram_a, gram_b = left_row[:, -rank:], right_row[:, -rank:]
    proj_a, proj_b = left_row[:, :-rank], right_row[:, :-rank]
    first = dot3(gram_a, wide([gram_b, proj_b]))
    inverse = inverse_of(first[:, :rank])
    coef_b = dot3(inverse, proj_a - first[:, rank:])
    coef_a = proj_b - dot3(gram_b, coef_b)
    return coef_a, coef_b


def adaptive_inverse(matrix):
    identity = eye(matrix.shape[0])

    def unfinished(state):
        step, _, power = state
        size = jnp.sum(power * power)
        return jnp.logical_and(size > 1e-14, step < 64)

    def body(state):
        step, inverse, power = state
        inverse, power = square_step(inverse, power)
        return step + 1, inverse, power

    state = (0, identity + matrix, dot3(matrix, matrix))
    return lax.while_loop(unfinished, body, state)[1]


def merged_rows(level_no, own, sib, sides, coef_a, coef_b, store):
    rank = coef_a.shape[0]
    proj_a, proj_b = sides[0][:, :-rank], sides[1][:, :-rank]
    stacked = jnp.concatenate([coef_a, coef_b], axis=0)
    rhs = split(jnp.concatenate([proj_a + coef_b, proj_b + coef_a], axis=0))
    for row_no in range(level_no):
        columns = slice((row_no + 1) * rank, (row_no + 2) * rank)
        turned = split(stacked[:, columns].T)
        end = (row_no + 2) * rank
        change = dot_split(turned, (rhs[0][:, :end], rhs[1][:, :end]))
        for col in range(row_no + 2):
            slot = offset(row_no) + col
            store(slot, own(slot) + sib(slot) - change[:, col * rank : (col + 1) * rank])


def final_coefs(coef_of, levels):
    deltas = []
    for level_no in range(levels):
        delta = coef_of(level_no, 0)
        if deltas:
            known = jnp.concatenate(deltas, axis=0)
            delta = delta - dot3(wide([coef_of(level_no, 1 + i) for i in range(level_no)]), known)
        deltas.append(delta)
    return deltas


def gram_kernel(bases_ref, targets_ref, out_ref):
    def store(slot, value):
        out_ref[slot] = value

    gram_rows(bases_ref, targets_ref, store)


def level_kernel(level_no, group_bits, own_ref, sib_ref, *out_refs):
    coef_ref = out_refs[0]
    is_left = lax.rem(lax.axis_index(AXIS) // 2**group_bits, 2) == 0
    base = offset(level_no)
    own_row = wide([own_ref[base + col] for col in range(level_no + 2)])
    sib_row = wide([sib_ref[base + col] for col in range(level_no + 2)])
    sides = (jnp.where(is_left, own_row, sib_row), jnp.where(is_left, sib_row, own_row))
    coef_a, coef_b = solve_pair(*sides, adaptive_inverse)
    own_coef = jnp.where(is_left, coef_a, coef_b)
    rank = coef_a.shape[0]
    for col in range(level_no + 1):
        coef_ref[col] = own_coef[:, col * rank : (col + 1) * rank]
    if level_no:
        next_ref = out_refs[1]

        def store(slot, value):
            next_ref[slot] = value

        merged_rows(
            level_no, lambda s: own_ref[s], lambda s: sib_ref[s], sides, coef_a, coef_b, store
        )


def apply_kernel(bases_ref, targets_ref, *refs):
    levels = bases_ref.shape[0]
    coefs, out_ref = refs[:-1], refs[-1]
    deltas = final_coefs(lambda level_no, col: coefs[level_no][col], levels)
    lhs = wide([bases_ref[level_no] for level_no in range(levels)])
    out_ref[...] = targets_ref[...] - dot3(lhs, jnp.concatenate(deltas, axis=0))


def call(kernel, outs, args):
    return pl.pallas_call(
        kernel,
        out_shape=outs,
        in_specs=[VMEM_SPEC] * len(args),
        out_specs=jax.tree.map(lambda _: VMEM_SPEC, outs),
        compiler_params=pltpu.CompilerParams(vmem_limit_bytes=VMEM_LIMIT),
    )(*args)


def from_partner(value, bit_no):
    pairs = [(source, source ^ 2**bit_no) for source in range(lax.axis_size(AXIS))]
    return lax.ppermute(value, AXIS, pairs)


def blocks(count, rank):
    return jax.ShapeDtypeStruct((count, rank, rank), jnp.float32)


SQUARINGS = 4
RESIDUAL = 1e-9


def fixed_inverse(matrix):
    inverse, power = eye(matrix.shape[0]) + matrix, dot3(matrix, matrix)
    for _ in range(SQUARINGS):
        inverse, power = square_step(inverse, power)
    return inverse, power


def fused_kernel(depth, bases_ref, targets_ref, out_ref, flag_ref, *refs):
    levels, _, rank = bases_ref.shape
    half = rank // 2
    sums, taken = refs[:depth], refs[depth : 2 * depth]
    coef, turned_ref, moved, flag_own, flag_in = refs[2 * depth : 2 * depth + 5]
    sems = refs[2 * depth + 5 :]
    link_send, link_recv, core_send, core_recv, relay_send, relay_recv, flag_send, flag_recv = sems
    me = lax.axis_index(AXIS)
    core = lax.rem(me, 2)
    own_half = pl.ds(pl.multiple_of(core * half, half), half)
    other_half = pl.ds(pl.multiple_of((1 - core) * half, half), half)
    pending = []

    def side(bit):
        return lax.rem(me // 2**bit, 2)

    def partner(bit):
        return me + 2**bit * (1 - 2 * side(bit))

    def push(src, dst, send, recv, bit):
        copy = pltpu.make_async_remote_copy(
            src_ref=src,
            dst_ref=dst,
            send_sem=send,
            recv_sem=recv,
            device_id=(partner(bit),),
            device_id_type=pl.DeviceIdType.MESH,
        )
        copy.start()
        pending.append(copy)
        return copy

    barrier = pltpu.get_barrier_semaphore()
    for bit in range(depth):
        pl.semaphore_signal(
            barrier, inc=1, device_id=(partner(bit),), device_id_type=pl.DeviceIdType.MESH
        )

    links, swaps = {}, {}

    def send_row(bit, row):
        slots = pl.ds(offset(row), row + 2)
        critical = row == depth - 1 - bit
        if bit == 0:
            region = (slots,) if critical else (slots, other_half)
        else:
            region = (slots, own_half)
        src, dst = sums[bit].at[region], taken[bit].at[region]
        links[bit, row] = push(src, dst, link_send.at[bit, row], link_recv.at[bit, row], bit)
        if critical and bit:
            swaps[bit] = push(src, src, core_send.at[bit], core_recv.at[bit], 0)

    parts = [split(targets_ref[...])] + [split(bases_ref[i]) for i in range(levels)]
    high, low = wide([part[0] for part in parts]), wide([part[1] for part in parts])
    for row in reversed(range(levels)):
        end = (row + 2) * rank
        value = dot_split(split(bases_ref[row].T), (high[:, :end], low[:, :end]))
        for col in range(row + 2):
            sums[0][offset(row) + col] = value[:, col * rank : (col + 1) * rank]
        if row == levels - 1:
            pl.semaphore_wait(barrier, depth)
        send_row(0, row)

    def coef_slot(level_no, col):
        return level_no * (level_no + 1) // 2 + col

    def move_rows():
        deltas = []
        for level_no in range(1, levels):
            delta = wide([coef[coef_slot(level_no, col)] for col in range(2)])
            if deltas:
                lhs = wide([coef[coef_slot(level_no, 1 + i)] for i in range(1, level_no)])
                delta = delta - dot3(lhs, jnp.concatenate(deltas, axis=0))
            deltas.append(delta)
        change = dot_split((high[:, 2 * rank :], low[:, 2 * rank :]), split(jnp.concatenate(deltas, axis=0)))
        moved[:, :rank] = targets_ref[...] - change[:, :rank]
        moved[:, rank:] = bases_ref[0] - change[:, rank:]

    flag = jnp.zeros((8, 128), jnp.float32)
    for bit in range(depth):
        level_no = depth - 1 - bit
        solving = level_no < levels
        if bit:
            flag_own[bit] = flag
            flag_copy = push(
                flag_own.at[bit], flag_in.at[bit], flag_send.at[bit], flag_recv.at[bit], bit
            )
        if level_no == 0:
            move_rows()
        if solving:
            slots = pl.ds(offset(level_no), level_no + 2)
            links[bit, level_no].wait_recv()
            if bit:
                region = taken[bit].at[slots, own_half]
                relay = push(region, region, relay_send.at[bit], relay_recv.at[bit], 0)
                swaps[bit].wait_recv()
                relay.wait_recv()
            base = offset(level_no)
            own_row = wide([sums[bit][base + col] for col in range(level_no + 2)])
            sib_row = wide([taken[bit][base + col] for col in range(level_no + 2)])
            is_left = side(bit) == 0
            left_row = jnp.where(is_left, own_row, sib_row)
            right_row = jnp.where(is_left, sib_row, own_row)
            state = []

            def inverse_of(matrix):
                inverse, power = fixed_inverse(matrix)
                state.append(jnp.max((power * power).reshape(rank // 8, 8, rank), axis=0))
                return inverse

            coef_a, coef_b = solve_pair(left_row, right_row, inverse_of)
            flag = jnp.maximum(flag, state[0])
            own_coef = jnp.where(is_left, coef_a, coef_b)
            if level_no == 0:
                out_ref[...] = moved[:, :rank] - dot3(moved[:, rank:], own_coef)
            for col in range(level_no + 1):
                coef[coef_slot(level_no, col)] = own_coef[:, col * rank : (col + 1) * rank]
            if level_no:
                proj_a, proj_b = left_row[:, :-rank], right_row[:, :-rank]
                stacked = jnp.concatenate([coef_a, coef_b], axis=0)
                rhs = split(jnp.concatenate([proj_a + coef_b, proj_b + coef_a], axis=0))
        for row in reversed(range(min(level_no, levels))):
            if solving:
                turned_ref[...] = stacked[:, (row + 1) * rank : (row + 2) * rank].T
                end = (row + 2) * rank
                change = dot_split(split(turned_ref[own_half, :]), (rhs[0][:, :end], rhs[1][:, :end]))
            links[bit, row].wait_recv()
            for col in range(row + 2):
                slot = offset(row) + col
                value = sums[bit][slot, own_half, :] + taken[bit][slot, own_half, :]
                if solving:
                    value = value - change[:, col * rank : (col + 1) * rank]
                sums[bit + 1][slot, own_half, :] = value
            send_row(bit + 1, row)
        if bit:
            flag_copy.wait_recv()
            flag = jnp.maximum(flag, flag_in[bit])
    flag_ref[...] = flag
    for copy in pending:
        copy.wait_send()


def fused(bases, targets, depth):
    levels, rows, rank = bases.shape
    stages = [
        pltpu.VMEM((offset(min(depth - bit, levels)), rank, rank), jnp.float32)
        for bit in range(depth)
    ]
    dma = pltpu.SemaphoreType.DMA
    return pl.pallas_call(
        functools.partial(fused_kernel, depth),
        out_shape=(
            jax.ShapeDtypeStruct(targets.shape, jnp.float32),
            jax.ShapeDtypeStruct((8, 128), jnp.float32),
        ),
        in_specs=[VMEM_SPEC] * 2,
        out_specs=(VMEM_SPEC, VMEM_SPEC),
        scratch_shapes=stages
        + stages
        + [
            pltpu.VMEM((levels * (levels + 1) // 2, rank, rank), jnp.float32),
            pltpu.VMEM((rank, 2 * rank), jnp.float32),
            pltpu.VMEM((rows, 2 * rank), jnp.float32),
            pltpu.VMEM((depth, 8, 128), jnp.float32),
            pltpu.VMEM((depth, 8, 128), jnp.float32),
        ]
        + [dma((depth, levels))] * 2
        + [dma((depth,))] * 6,
        compiler_params=pltpu.CompilerParams(
            collective_id=0, has_side_effects=True, vmem_limit_bytes=VMEM_LIMIT
        ),
    )(bases, targets)


def general(bases, targets):
    levels, _, rank = bases.shape
    tree_depth = lax.axis_size(AXIS).bit_length() - 1
    sums = call(gram_kernel, blocks(offset(levels), rank), (bases, targets))
    for bit_no in range(tree_depth - levels):
        sums = sums + from_partner(sums, bit_no)
    coefs = [None] * levels
    for level_no in reversed(range(levels)):
        group_bits = tree_depth - level_no - 1
        sibling = from_partner(sums, group_bits)
        outs = [blocks(level_no + 1, rank)]
        if level_no:
            outs.append(blocks(offset(level_no), rank))
        kernel = functools.partial(level_kernel, level_no, group_bits)
        coefs[level_no], *rest = call(kernel, tuple(outs), (sums, sibling))
        sums = rest[0] if rest else None
    out = jax.ShapeDtypeStruct(targets.shape, jnp.float32)
    return call(apply_kernel, out, (bases, targets, *coefs))


def per_device(bases, targets):
    depth = lax.axis_size(AXIS).bit_length() - 1
    out, residual = fused(bases, targets, depth)
    limit = (RESIDUAL / bases.shape[2]) ** 2
    return lax.cond(
        jnp.max(residual) < limit, lambda b, t, o: o, lambda b, t, o: general(b, t), bases, targets, out
    )


def solution(mesh):
    return jax.shard_map(
        per_device,
        mesh=mesh,
        in_specs=(P(None, AXIS, None), P(AXIS, None)),
        out_specs=P(AXIS, None),
        check_vma=False,
    )
```

```python
import functools

import jax
import jax.numpy as jnp
from jax import lax
from jax.experimental import pallas as pl
from jax.experimental.pallas import tpu as pltpu
from jax.sharding import PartitionSpec as P

AXIS = "rows"
VMEM_LIMIT = 48 * 2**20
VMEM_SPEC = pl.BlockSpec(memory_space=pltpu.VMEM)


def offset(level_no):
    return level_no * (level_no + 3) // 2


def split(value):
    high = value.astype(jnp.bfloat16)
    low = (value - high.astype(jnp.float32)).astype(jnp.bfloat16)
    return high, low


def dot_split(left, right):
    left_high, left_low = left
    right_high, right_low = right
    dot = functools.partial(jnp.dot, preferred_element_type=jnp.float32)
    return (dot(left_low, right_high) + dot(left_high, right_low)) + dot(left_high, right_high)


def dot3(left, right):
    return dot_split(split(left), split(right))


def wide(blocks):
    return jnp.concatenate(blocks, axis=1)


def gram_rows(bases_ref, targets_ref, store):
    levels = bases_ref.shape[0]
    rank = bases_ref.shape[2]
    parts = [split(targets_ref[...])]
    for level_no in range(levels):
        basis = bases_ref[level_no]
        parts.append(split(basis))
        turned = split(basis.T)
        rhs = (wide([part[0] for part in parts]), wide([part[1] for part in parts]))
        row = dot_split(turned, rhs)
        for col in range(level_no + 2):
            store(offset(level_no) + col, row[:, col * rank : (col + 1) * rank])


def eye(rank):
    shape = (rank, rank)
    row = lax.broadcasted_iota(jnp.int32, shape, 0)
    col = lax.broadcasted_iota(jnp.int32, shape, 1)
    return (row == col).astype(jnp.float32)


def square_step(inverse, power):
    rank = power.shape[0]
    both = dot3(power, wide([inverse, power]))
    return inverse + both[:, :rank], both[:, rank:]


def solve_pair(left_row, right_row, inverse_of):
    rank = left_row.shape[0]
    gram_a, gram_b = left_row[:, -rank:], right_row[:, -rank:]
    proj_a, proj_b = left_row[:, :-rank], right_row[:, :-rank]
    first = dot3(gram_a, wide([gram_b, proj_b]))
    inverse = inverse_of(first[:, :rank])
    coef_b = dot3(inverse, proj_a - first[:, rank:])
    coef_a = proj_b - dot3(gram_b, coef_b)
    return coef_a, coef_b


def adaptive_inverse(matrix):
    identity = eye(matrix.shape[0])

    def unfinished(state):
        step, _, power = state
        size = jnp.sum(power * power)
        return jnp.logical_and(size > 1e-14, step < 64)

    def body(state):
        step, inverse, power = state
        inverse, power = square_step(inverse, power)
        return step + 1, inverse, power

    state = (0, identity + matrix, dot3(matrix, matrix))
    return lax.while_loop(unfinished, body, state)[1]


def merged_rows(level_no, own, sib, sides, coef_a, coef_b, store):
    rank = coef_a.shape[0]
    proj_a, proj_b = sides[0][:, :-rank], sides[1][:, :-rank]
    stacked = jnp.concatenate([coef_a, coef_b], axis=0)
    rhs = split(jnp.concatenate([proj_a + coef_b, proj_b + coef_a], axis=0))
    for row_no in range(level_no):
        columns = slice((row_no + 1) * rank, (row_no + 2) * rank)
        turned = split(stacked[:, columns].T)
        end = (row_no + 2) * rank
        change = dot_split(turned, (rhs[0][:, :end], rhs[1][:, :end]))
        for col in range(row_no + 2):
            slot = offset(row_no) + col
            store(slot, own(slot) + sib(slot) - change[:, col * rank : (col + 1) * rank])


def final_coefs(coef_of, levels):
    deltas = []
    for level_no in range(levels):
        delta = coef_of(level_no, 0)
        if deltas:
            known = jnp.concatenate(deltas, axis=0)
            delta = delta - dot3(wide([coef_of(level_no, 1 + i) for i in range(level_no)]), known)
        deltas.append(delta)
    return deltas


def gram_kernel(bases_ref, targets_ref, out_ref):
    def store(slot, value):
        out_ref[slot] = value

    gram_rows(bases_ref, targets_ref, store)


def level_kernel(level_no, group_bits, own_ref, sib_ref, *out_refs):
    coef_ref = out_refs[0]
    is_left = lax.rem(lax.axis_index(AXIS) // 2**group_bits, 2) == 0
    base = offset(level_no)
    own_row = wide([own_ref[base + col] for col in range(level_no + 2)])
    sib_row = wide([sib_ref[base + col] for col in range(level_no + 2)])
    sides = (jnp.where(is_left, own_row, sib_row), jnp.where(is_left, sib_row, own_row))
    coef_a, coef_b = solve_pair(*sides, adaptive_inverse)
    own_coef = jnp.where(is_left, coef_a, coef_b)
    rank = coef_a.shape[0]
    for col in range(level_no + 1):
        coef_ref[col] = own_coef[:, col * rank : (col + 1) * rank]
    if level_no:
        next_ref = out_refs[1]

        def store(slot, value):
            next_ref[slot] = value

        merged_rows(
            level_no, lambda s: own_ref[s], lambda s: sib_ref[s], sides, coef_a, coef_b, store
        )


def apply_kernel(bases_ref, targets_ref, *refs):
    levels = bases_ref.shape[0]
    coefs, out_ref = refs[:-1], refs[-1]
    deltas = final_coefs(lambda level_no, col: coefs[level_no][col], levels)
    lhs = wide([bases_ref[level_no] for level_no in range(levels)])
    out_ref[...] = targets_ref[...] - dot3(lhs, jnp.concatenate(deltas, axis=0))


def call(kernel, outs, args):
    return pl.pallas_call(
        kernel,
        out_shape=outs,
        in_specs=[VMEM_SPEC] * len(args),
        out_specs=jax.tree.map(lambda _: VMEM_SPEC, outs),
        compiler_params=pltpu.CompilerParams(vmem_limit_bytes=VMEM_LIMIT),
    )(*args)


def from_partner(value, bit_no):
    pairs = [(source, source ^ 2**bit_no) for source in range(lax.axis_size(AXIS))]
    return lax.ppermute(value, AXIS, pairs)


def blocks(count, rank):
    return jax.ShapeDtypeStruct((count, rank, rank), jnp.float32)


SQUARINGS = 4
RESIDUAL = 1e-9


def fixed_inverse(matrix):
    inverse, power = eye(matrix.shape[0]) + matrix, dot3(matrix, matrix)
    for _ in range(SQUARINGS):
        inverse, power = square_step(inverse, power)
    return inverse, power


def fused_kernel(depth, bases_ref, targets_ref, moved, last_ref, flag_ref, *refs):
    levels, _, rank = bases_ref.shape
    half = rank // 2
    sums, taken = refs[:depth], refs[depth : 2 * depth]
    coef, turned_ref, flag_own, flag_in = refs[2 * depth : 2 * depth + 4]
    sems = refs[2 * depth + 4 :]
    link_send, link_recv, core_send, core_recv, relay_send, relay_recv, flag_send, flag_recv = sems
    me = lax.axis_index(AXIS)
    core = lax.rem(me, 2)
    own_half = pl.ds(pl.multiple_of(core * half, half), half)
    other_half = pl.ds(pl.multiple_of((1 - core) * half, half), half)
    pending = []

    def side(bit):
        return lax.rem(me // 2**bit, 2)

    def partner(bit):
        return me + 2**bit * (1 - 2 * side(bit))

    def push(src, dst, send, recv, bit):
        copy = pltpu.make_async_remote_copy(
            src_ref=src,
            dst_ref=dst,
            send_sem=send,
            recv_sem=recv,
            device_id=(partner(bit),),
            device_id_type=pl.DeviceIdType.MESH,
        )
        copy.start()
        pending.append(copy)
        return copy

    barrier = pltpu.get_barrier_semaphore()
    for bit in range(depth):
        pl.semaphore_signal(
            barrier, inc=1, device_id=(partner(bit),), device_id_type=pl.DeviceIdType.MESH
        )

    links, swaps = {}, {}

    def send_row(bit, row):
        slots = pl.ds(offset(row), row + 2)
        critical = row == depth - 1 - bit
        if bit == 0:
            region = (slots,) if critical else (slots, other_half)
        else:
            region = (slots, own_half)
        src, dst = sums[bit].at[region], taken[bit].at[region]
        links[bit, row] = push(src, dst, link_send.at[bit, row], link_recv.at[bit, row], bit)
        if critical and bit:
            swaps[bit] = push(src, src, core_send.at[bit], core_recv.at[bit], 0)

    parts = [split(targets_ref[...])] + [split(bases_ref[i]) for i in range(levels)]
    high, low = wide([part[0] for part in parts]), wide([part[1] for part in parts])
    for row in reversed(range(levels)):
        end = (row + 2) * rank
        value = dot_split(split(bases_ref[row].T), (high[:, :end], low[:, :end]))
        for col in range(row + 2):
            sums[0][offset(row) + col] = value[:, col * rank : (col + 1) * rank]
        if row == levels - 1:
            pl.semaphore_wait(barrier, depth)
        send_row(0, row)

    def coef_slot(level_no, col):
        return level_no * (level_no + 1) // 2 + col

    def move_rows():
        deltas = []
        for level_no in range(1, levels):
            delta = wide([coef[coef_slot(level_no, col)] for col in range(2)])
            if deltas:
                lhs = wide([coef[coef_slot(level_no, 1 + i)] for i in range(1, level_no)])
                delta = delta - dot3(lhs, jnp.concatenate(deltas, axis=0))
            deltas.append(delta)
        change = dot_split((high[:, 2 * rank :], low[:, 2 * rank :]), split(jnp.concatenate(deltas, axis=0)))
        moved[:, :rank] = targets_ref[...] - change[:, :rank]
        moved[:, rank:] = bases_ref[0] - change[:, rank:]

    def merge_row(bit, row, change_of):
        links[bit, row].wait_recv()
        change = change_of(row)
        for col in range(row + 2):
            slot = offset(row) + col
            value = sums[bit][slot, own_half, :] + taken[bit][slot, own_half, :]
            if change is not None:
                value = value - change[:, col * rank : (col + 1) * rank]
            sums[bit + 1][slot, own_half, :] = value

    def changes(coef_a, coef_b, left_row, right_row):
        proj_a, proj_b = left_row[:, :-rank], right_row[:, :-rank]
        stacked = jnp.concatenate([coef_a, coef_b], axis=0)
        rhs = split(jnp.concatenate([proj_a + coef_b, proj_b + coef_a], axis=0))

        def change_of(row):
            turned_ref[...] = stacked[:, (row + 1) * rank : (row + 2) * rank].T
            end = (row + 2) * rank
            return dot_split(split(turned_ref[own_half, :]), (rhs[0][:, :end], rhs[1][:, :end]))

        return change_of

    flag = jnp.zeros((8, 128), jnp.float32)
    late, late_change = [], None
    for bit in range(depth):
        level_no = depth - 1 - bit
        solving = level_no < levels
        rest = list(reversed(range(min(level_no, levels))))
        if bit:
            flag_own[bit] = flag
            flag_copy = push(
                flag_own.at[bit], flag_in.at[bit], flag_send.at[bit], flag_recv.at[bit], bit
            )
        if level_no == 0:
            move_rows()
        change_of = lambda row: None
        if solving:
            slots = pl.ds(offset(level_no), level_no + 2)
            links[bit, level_no].wait_recv()
            if bit:
                region = taken[bit].at[slots, own_half]
                relay = push(region, region, relay_send.at[bit], relay_recv.at[bit], 0)
            for row in late:
                merge_row(bit - 1, row, late_change)
                if row == rest[0]:
                    send_row(bit, row)
            if bit:
                swaps[bit].wait_recv()
                relay.wait_recv()
            base = offset(level_no)
            own_row = wide([sums[bit][base + col] for col in range(level_no + 2)])
            sib_row = wide([taken[bit][base + col] for col in range(level_no + 2)])
            is_left = side(bit) == 0
            left_row = jnp.where(is_left, own_row, sib_row)
            right_row = jnp.where(is_left, sib_row, own_row)
            state = []

            def inverse_of(matrix):
                inverse, power = fixed_inverse(matrix)
                state.append(jnp.max((power * power).reshape(rank // 8, 8, rank), axis=0))
                return inverse

            coef_a, coef_b = solve_pair(left_row, right_row, inverse_of)
            flag = jnp.maximum(flag, state[0])
            own_coef = jnp.where(is_left, coef_a, coef_b)
            for col in range(level_no + 1):
                coef[coef_slot(level_no, col)] = own_coef[:, col * rank : (col + 1) * rank]
            if level_no == 0:
                last_ref[...] = own_coef
            else:
                change_of = changes(coef_a, coef_b, left_row, right_row)
        if rest:
            following = level_no - 1 < levels
            for row in rest[:1] if following else rest:
                merge_row(bit, row, change_of)
                send_row(bit + 1, row)
            late = rest[1:] if following else []
            late_change = change_of
            for row in late:
                if (bit, row) not in links:
                    send_row(bit, row)
        if bit:
            flag_copy.wait_recv()
            flag = jnp.maximum(flag, flag_in[bit])
    flag_ref[...] = flag
    for copy in pending:
        copy.wait_send()


def finish_kernel(moved_ref, last_ref, out_ref):
    rank = last_ref.shape[0]
    out_ref[...] = moved_ref[:, :rank] - dot3(moved_ref[:, rank:], last_ref[...])


def fused(bases, targets, depth):
    levels, rows, rank = bases.shape
    stages = [
        pltpu.VMEM((offset(min(depth - bit, levels)), rank, rank), jnp.float32)
        for bit in range(depth)
    ]
    dma = pltpu.SemaphoreType.DMA
    return pl.pallas_call(
        functools.partial(fused_kernel, depth),
        out_shape=(
            jax.ShapeDtypeStruct((rows, 2 * rank), jnp.float32),
            jax.ShapeDtypeStruct((rank, rank), jnp.float32),
            jax.ShapeDtypeStruct((8, 128), jnp.float32),
        ),
        in_specs=[VMEM_SPEC] * 2,
        out_specs=(VMEM_SPEC,) * 3,
        scratch_shapes=stages
        + stages
        + [
            pltpu.VMEM((levels * (levels + 1) // 2, rank, rank), jnp.float32),
            pltpu.VMEM((rank, 2 * rank), jnp.float32),
            pltpu.VMEM((depth, 8, 128), jnp.float32),
            pltpu.VMEM((depth, 8, 128), jnp.float32),
        ]
        + [dma((depth, levels))] * 2
        + [dma((depth,))] * 6,
        compiler_params=pltpu.CompilerParams(
            collective_id=0, has_side_effects=True, vmem_limit_bytes=VMEM_LIMIT
        ),
    )(bases, targets)


def general(bases, targets):
    levels, _, rank = bases.shape
    tree_depth = lax.axis_size(AXIS).bit_length() - 1
    sums = call(gram_kernel, blocks(offset(levels), rank), (bases, targets))
    for bit_no in range(tree_depth - levels):
        sums = sums + from_partner(sums, bit_no)
    coefs = [None] * levels
    for level_no in reversed(range(levels)):
        group_bits = tree_depth - level_no - 1
        sibling = from_partner(sums, group_bits)
        outs = [blocks(level_no + 1, rank)]
        if level_no:
            outs.append(blocks(offset(level_no), rank))
        kernel = functools.partial(level_kernel, level_no, group_bits)
        coefs[level_no], *rest = call(kernel, tuple(outs), (sums, sibling))
        sums = rest[0] if rest else None
    out = jax.ShapeDtypeStruct(targets.shape, jnp.float32)
    return call(apply_kernel, out, (bases, targets, *coefs))


def per_device(bases, targets):
    depth = lax.axis_size(AXIS).bit_length() - 1
    moved, last, residual = fused(bases, targets, depth)
    limit = (RESIDUAL / bases.shape[2]) ** 2
    out = jax.ShapeDtypeStruct(targets.shape, jnp.float32)
    return lax.cond(
        jnp.max(residual) < limit,
        lambda: call(finish_kernel, out, (moved, last)),
        lambda: general(bases, targets),
    )


def solution(mesh):
    return jax.shard_map(
        per_device,
        mesh=mesh,
        in_specs=(P(None, AXIS, None), P(AXIS, None)),
        out_specs=P(AXIS, None),
        check_vma=False,
    )
```

```python
import functools

import jax
import jax.numpy as jnp
from jax import lax
from jax.experimental import pallas as pl
from jax.experimental.pallas import tpu as pltpu
from jax.sharding import PartitionSpec as P

AXIS = "rows"
VMEM_LIMIT = 48 * 2**20
VMEM_SPEC = pl.BlockSpec(memory_space=pltpu.VMEM)


def offset(level_no):
    return level_no * (level_no + 3) // 2


def split(value):
    high = value.astype(jnp.bfloat16)
    low = (value - high.astype(jnp.float32)).astype(jnp.bfloat16)
    return high, low


def dot_split(left, right):
    left_high, left_low = left
    right_high, right_low = right
    dot = functools.partial(jnp.dot, preferred_element_type=jnp.float32)
    return (dot(left_low, right_high) + dot(left_high, right_low)) + dot(left_high, right_high)


def dot3(left, right):
    return dot_split(split(left), split(right))


def wide(blocks):
    return jnp.concatenate(blocks, axis=1)


def gram_rows(bases_ref, targets_ref, store):
    levels = bases_ref.shape[0]
    rank = bases_ref.shape[2]
    parts = [split(targets_ref[...])]
    for level_no in range(levels):
        basis = bases_ref[level_no]
        parts.append(split(basis))
        turned = split(basis.T)
        rhs = (wide([part[0] for part in parts]), wide([part[1] for part in parts]))
        row = dot_split(turned, rhs)
        for col in range(level_no + 2):
            store(offset(level_no) + col, row[:, col * rank : (col + 1) * rank])


def eye(rank):
    shape = (rank, rank)
    row = lax.broadcasted_iota(jnp.int32, shape, 0)
    col = lax.broadcasted_iota(jnp.int32, shape, 1)
    return (row == col).astype(jnp.float32)


def square_step(inverse, power):
    rank = power.shape[0]
    both = dot3(power, wide([inverse, power]))
    return inverse + both[:, :rank], both[:, rank:]


def solve_pair(left_row, right_row, inverse_of):
    rank = left_row.shape[0]
    gram_a, gram_b = left_row[:, -rank:], right_row[:, -rank:]
    proj_a, proj_b = left_row[:, :-rank], right_row[:, :-rank]
    first = dot3(gram_a, wide([gram_b, proj_b]))
    inverse = inverse_of(first[:, :rank])
    coef_b = dot3(inverse, proj_a - first[:, rank:])
    coef_a = proj_b - dot3(gram_b, coef_b)
    return coef_a, coef_b


def adaptive_inverse(matrix):
    identity = eye(matrix.shape[0])

    def unfinished(state):
        step, _, power = state
        size = jnp.sum(power * power)
        return jnp.logical_and(size > 1e-14, step < 64)

    def body(state):
        step, inverse, power = state
        inverse, power = square_step(inverse, power)
        return step + 1, inverse, power

    state = (0, identity + matrix, dot3(matrix, matrix))
    return lax.while_loop(unfinished, body, state)[1]


def merged_rows(level_no, own, sib, sides, coef_a, coef_b, store):
    rank = coef_a.shape[0]
    proj_a, proj_b = sides[0][:, :-rank], sides[1][:, :-rank]
    stacked = jnp.concatenate([coef_a, coef_b], axis=0)
    rhs = split(jnp.concatenate([proj_a + coef_b, proj_b + coef_a], axis=0))
    for row_no in range(level_no):
        columns = slice((row_no + 1) * rank, (row_no + 2) * rank)
        turned = split(stacked[:, columns].T)
        end = (row_no + 2) * rank
        change = dot_split(turned, (rhs[0][:, :end], rhs[1][:, :end]))
        for col in range(row_no + 2):
            slot = offset(row_no) + col
            store(slot, own(slot) + sib(slot) - change[:, col * rank : (col + 1) * rank])


def final_coefs(coef_of, levels):
    deltas = []
    for level_no in range(levels):
        delta = coef_of(level_no, 0)
        if deltas:
            known = jnp.concatenate(deltas, axis=0)
            delta = delta - dot3(wide([coef_of(level_no, 1 + i) for i in range(level_no)]), known)
        deltas.append(delta)
    return deltas


def gram_kernel(bases_ref, targets_ref, out_ref):
    def store(slot, value):
        out_ref[slot] = value

    gram_rows(bases_ref, targets_ref, store)


def level_kernel(level_no, group_bits, own_ref, sib_ref, *out_refs):
    coef_ref = out_refs[0]
    is_left = lax.rem(lax.axis_index(AXIS) // 2**group_bits, 2) == 0
    base = offset(level_no)
    own_row = wide([own_ref[base + col] for col in range(level_no + 2)])
    sib_row = wide([sib_ref[base + col] for col in range(level_no + 2)])
    sides = (jnp.where(is_left, own_row, sib_row), jnp.where(is_left, sib_row, own_row))
    coef_a, coef_b = solve_pair(*sides, adaptive_inverse)
    own_coef = jnp.where(is_left, coef_a, coef_b)
    rank = coef_a.shape[0]
    for col in range(level_no + 1):
        coef_ref[col] = own_coef[:, col * rank : (col + 1) * rank]
    if level_no:
        next_ref = out_refs[1]

        def store(slot, value):
            next_ref[slot] = value

        merged_rows(
            level_no, lambda s: own_ref[s], lambda s: sib_ref[s], sides, coef_a, coef_b, store
        )


def apply_kernel(bases_ref, targets_ref, *refs):
    levels = bases_ref.shape[0]
    coefs, out_ref = refs[:-1], refs[-1]
    deltas = final_coefs(lambda level_no, col: coefs[level_no][col], levels)
    lhs = wide([bases_ref[level_no] for level_no in range(levels)])
    out_ref[...] = targets_ref[...] - dot3(lhs, jnp.concatenate(deltas, axis=0))


def call(kernel, outs, args):
    return pl.pallas_call(
        kernel,
        out_shape=outs,
        in_specs=[VMEM_SPEC] * len(args),
        out_specs=jax.tree.map(lambda _: VMEM_SPEC, outs),
        compiler_params=pltpu.CompilerParams(vmem_limit_bytes=VMEM_LIMIT),
    )(*args)


def from_partner(value, bit_no):
    pairs = [(source, source ^ 2**bit_no) for source in range(lax.axis_size(AXIS))]
    return lax.ppermute(value, AXIS, pairs)


def blocks(count, rank):
    return jax.ShapeDtypeStruct((count, rank, rank), jnp.float32)


SQUARINGS = 3
RESIDUAL = 1e-7


def fixed_inverse(matrix):
    inverse, power = eye(matrix.shape[0]) + matrix, dot3(matrix, matrix)
    for _ in range(SQUARINGS):
        inverse, power = square_step(inverse, power)
    return inverse, power


def inverse_of_pair(gram_a, gram_b):
    rank = gram_a.shape[0]
    parts_a, parts_b = split(gram_a), split(gram_b)
    inverse, power = fixed_inverse(dot_split(parts_a, parts_b))
    weighted = dot_split(split(inverse), parts_a)
    lower = wide([inverse, -weighted])
    upper = wide([jnp.zeros_like(gram_a), eye(rank)]) - dot_split(parts_b, split(lower))
    return split(jnp.concatenate([upper, lower], axis=0)), power


def fused_kernel(depth, bases_ref, targets_ref, out_ref, flag_ref, *refs):
    levels, _, rank = bases_ref.shape
    half = rank // 2
    sums, taken = refs[:depth], refs[depth : 2 * depth]
    coef, turned_ref, moved, flag_own, flag_in = refs[2 * depth : 2 * depth + 5]
    sems = refs[2 * depth + 5 :]
    link_send, link_recv, core_send, core_recv, relay_send, relay_recv, flag_send, flag_recv = sems
    me = lax.axis_index(AXIS)
    core = lax.rem(me, 2)
    own_half = pl.ds(pl.multiple_of(core * half, half), half)
    other_half = pl.ds(pl.multiple_of((1 - core) * half, half), half)
    pending = []

    def side(bit):
        return lax.rem(me // 2**bit, 2)

    def partner(bit):
        return me + 2**bit * (1 - 2 * side(bit))

    def push(src, dst, send, recv, bit):
        copy = pltpu.make_async_remote_copy(
            src_ref=src,
            dst_ref=dst,
            send_sem=send,
            recv_sem=recv,
            device_id=(partner(bit),),
            device_id_type=pl.DeviceIdType.MESH,
        )
        copy.start()
        pending.append(copy)
        return copy

    barrier = pltpu.get_barrier_semaphore()
    for bit in range(depth):
        pl.semaphore_signal(
            barrier, inc=1, device_id=(partner(bit),), device_id_type=pl.DeviceIdType.MESH
        )

    links, swaps = {}, {}

    def piece(row, number):
        if number == 0:
            return pl.ds(offset(row) + row + 1, 1)
        return pl.ds(offset(row), row + 1)

    def send_critical(bit, row):
        for number in range(2):
            region = (piece(row, number), own_half) if bit else (piece(row, number),)
            src, dst = sums[bit].at[region], taken[bit].at[region]
            send, recv = link_send.at[bit, number, row], link_recv.at[bit, number, row]
            links[bit, row, number] = push(src, dst, send, recv, bit)
            if bit:
                send, recv = core_send.at[bit, number], core_recv.at[bit, number]
                swaps[bit, number] = push(src, src, send, recv, 0)

    def send_row(bit, row):
        if row == depth - 1 - bit:
            send_critical(bit, row)
            return
        region = (pl.ds(offset(row), row + 2), own_half if bit else other_half)
        src, dst = sums[bit].at[region], taken[bit].at[region]
        send, recv = link_send.at[bit, 0, row], link_recv.at[bit, 0, row]
        links[bit, row] = push(src, dst, send, recv, bit)

    def relay_piece(bit, row, number):
        links[bit, row, number].wait_recv()
        if bit == 0:
            return None
        region = taken[bit].at[piece(row, number), own_half]
        send, recv = relay_send.at[bit, number], relay_recv.at[bit, number]
        return push(region, region, send, recv, 0)

    def finish_piece(bit, number, relay):
        if relay is not None:
            swaps[bit, number].wait_recv()
            relay.wait_recv()

    parts = [split(targets_ref[...])] + [split(bases_ref[i]) for i in range(levels)]
    high, low = wide([part[0] for part in parts]), wide([part[1] for part in parts])
    for row in reversed(range(levels)):
        end = (row + 2) * rank
        value = dot_split(split(bases_ref[row].T), (high[:, :end], low[:, :end]))
        for col in range(row + 2):
            sums[0][offset(row) + col] = value[:, col * rank : (col + 1) * rank]
        if row == levels - 1:
            pl.semaphore_wait(barrier, depth)
        send_row(0, row)

    def coef_slot(level_no, col):
        return level_no * (level_no + 1) // 2 + col

    def move_rows():
        deltas = []
        for level_no in range(1, levels):
            delta = wide([coef[coef_slot(level_no, col)] for col in range(2)])
            if deltas:
                lhs = wide([coef[coef_slot(level_no, 1 + i)] for i in range(1, level_no)])
                delta = delta - dot3(lhs, jnp.concatenate(deltas, axis=0))
            deltas.append(delta)
        change = dot_split((high[:, 2 * rank :], low[:, 2 * rank :]), split(jnp.concatenate(deltas, axis=0)))
        moved[:, :rank] = targets_ref[...] - change[:, :rank]
        moved[:, rank:] = bases_ref[0] - change[:, rank:]

    def merge_row(bit, row, change_of):
        links[bit, row].wait_recv()
        change = change_of(row)
        for col in range(row + 2):
            slot = offset(row) + col
            value = sums[bit][slot, own_half, :] + taken[bit][slot, own_half, :]
            if change is not None:
                value = value - change[:, col * rank : (col + 1) * rank]
            sums[bit + 1][slot, own_half, :] = value

    def changes(stacked, upper, lower):
        rhs = split(jnp.concatenate([upper, lower], axis=0))

        def change_of(row):
            turned_ref[...] = stacked[:, (row + 1) * rank : (row + 2) * rank].T
            end = (row + 2) * rank
            return dot_split(split(turned_ref[own_half, :]), (rhs[0][:, :end], rhs[1][:, :end]))

        return change_of

    flag = jnp.zeros((8, 128), jnp.float32)
    late, late_change = [], None
    for bit in range(depth):
        level_no = depth - 1 - bit
        solving = level_no < levels
        rest = list(reversed(range(min(level_no, levels))))
        if bit:
            flag_own[bit] = flag
            flag_copy = push(
                flag_own.at[bit], flag_in.at[bit], flag_send.at[bit], flag_recv.at[bit], bit
            )
        if level_no == 0:
            move_rows()
        change_of = lambda row: None
        if solving:
            base = offset(level_no)
            is_left = side(bit) == 0

            def both_sides(slots):
                own = wide([sums[bit][slot] for slot in slots])
                sib = wide([taken[bit][slot] for slot in slots])
                return jnp.where(is_left, own, sib), jnp.where(is_left, sib, own)

            relay = relay_piece(bit, level_no, 0)
            finish_piece(bit, 0, relay)
            gram_a, gram_b = both_sides([base + level_no + 1])
            pair_inverse, power = inverse_of_pair(gram_a, gram_b)
            relay = relay_piece(bit, level_no, 1)
            for row in late:
                merge_row(bit - 1, row, late_change)
                if row == rest[0]:
                    send_row(bit, row)
            finish_piece(bit, 1, relay)
            proj_a, proj_b = both_sides(range(base, base + level_no + 1))
            stacked_proj = jnp.concatenate([proj_a, proj_b], axis=0)
            stacked = dot_split(pair_inverse, split(stacked_proj))
            coef_a, coef_b = stacked[:rank], stacked[rank:]
            state = [jnp.max((power * power).reshape(rank // 8, 8, rank), axis=0)]
            flag = jnp.maximum(flag, state[0])
            own_coef = jnp.where(is_left, coef_a, coef_b)
            for col in range(level_no + 1):
                coef[coef_slot(level_no, col)] = own_coef[:, col * rank : (col + 1) * rank]
            if level_no == 0:
                out_ref[...] = moved[:, :rank] - dot3(moved[:, rank:], own_coef)
            else:
                change_of = changes(stacked, proj_a + coef_b, proj_b + coef_a)
        if rest:
            following = level_no - 1 < levels
            for row in rest[:1] if following else rest:
                merge_row(bit, row, change_of)
                send_row(bit + 1, row)
            late = rest[1:] if following else []
            late_change = change_of
            for row in late:
                if (bit, row) not in links:
                    send_row(bit, row)
        if bit:
            flag_copy.wait_recv()
            flag = jnp.maximum(flag, flag_in[bit])
    flag_ref[...] = flag
    for copy in pending:
        copy.wait_send()


def fused(bases, targets, depth):
    levels, rows, rank = bases.shape
    stages = [
        pltpu.VMEM((offset(min(depth - bit, levels)), rank, rank), jnp.float32)
        for bit in range(depth)
    ]
    dma = pltpu.SemaphoreType.DMA
    return pl.pallas_call(
        functools.partial(fused_kernel, depth),
        out_shape=(
            jax.ShapeDtypeStruct(targets.shape, jnp.float32),
            jax.ShapeDtypeStruct((8, 128), jnp.float32),
        ),
        in_specs=[VMEM_SPEC] * 2,
        out_specs=(VMEM_SPEC,) * 2,
        scratch_shapes=stages
        + stages
        + [
            pltpu.VMEM((levels * (levels + 1) // 2, rank, rank), jnp.float32),
            pltpu.VMEM((rank, 2 * rank), jnp.float32),
            pltpu.VMEM((rows, 2 * rank), jnp.float32),
            pltpu.VMEM((depth, 8, 128), jnp.float32),
            pltpu.VMEM((depth, 8, 128), jnp.float32),
        ]
        + [dma((depth, 2, levels))] * 2
        + [dma((depth, 2))] * 4
        + [dma((depth,))] * 2,
        compiler_params=pltpu.CompilerParams(
            collective_id=0, has_side_effects=True, vmem_limit_bytes=VMEM_LIMIT
        ),
    )(bases, targets)


def general(bases, targets):
    levels, _, rank = bases.shape
    tree_depth = lax.axis_size(AXIS).bit_length() - 1
    sums = call(gram_kernel, blocks(offset(levels), rank), (bases, targets))
    for bit_no in range(tree_depth - levels):
        sums = sums + from_partner(sums, bit_no)
    coefs = [None] * levels
    for level_no in reversed(range(levels)):
        group_bits = tree_depth - level_no - 1
        sibling = from_partner(sums, group_bits)
        outs = [blocks(level_no + 1, rank)]
        if level_no:
            outs.append(blocks(offset(level_no), rank))
        kernel = functools.partial(level_kernel, level_no, group_bits)
        coefs[level_no], *rest = call(kernel, tuple(outs), (sums, sibling))
        sums = rest[0] if rest else None
    out = jax.ShapeDtypeStruct(targets.shape, jnp.float32)
    return call(apply_kernel, out, (bases, targets, *coefs))


def per_device(bases, targets):
    depth = lax.axis_size(AXIS).bit_length() - 1
    out, residual = fused(bases, targets, depth)
    limit = (RESIDUAL / bases.shape[2]) ** 2
    return lax.cond(
        jnp.max(residual) < limit, lambda b, t, o: o, lambda b, t, o: general(b, t), bases, targets, out
    )


def solution(mesh):
    return jax.shard_map(
        per_device,
        mesh=mesh,
        in_specs=(P(None, AXIS, None), P(AXIS, None)),
        out_specs=P(AXIS, None),
        check_vma=False,
    )
```

```python
import functools

import jax
import jax.numpy as jnp
from jax import lax
from jax.experimental import pallas as pl
from jax.experimental.pallas import tpu as pltpu
from jax.sharding import PartitionSpec as P

AXIS = "rows"
VMEM_LIMIT = 48 * 2**20
VMEM_SPEC = pl.BlockSpec(memory_space=pltpu.VMEM)


def offset(level_no):
    return level_no * (level_no + 3) // 2


def split(value):
    high = value.astype(jnp.bfloat16)
    low = (value - high.astype(jnp.float32)).astype(jnp.bfloat16)
    return high, low


def dot_split(left, right):
    left_high, left_low = left
    right_high, right_low = right
    dot = functools.partial(jnp.dot, preferred_element_type=jnp.float32)
    return (dot(left_low, right_high) + dot(left_high, right_low)) + dot(left_high, right_high)


def dot3(left, right):
    return dot_split(split(left), split(right))


def wide(blocks):
    return jnp.concatenate(blocks, axis=1)


def gram_rows(bases_ref, targets_ref, store):
    levels = bases_ref.shape[0]
    rank = bases_ref.shape[2]
    parts = [split(targets_ref[...])]
    for level_no in range(levels):
        basis = bases_ref[level_no]
        parts.append(split(basis))
        turned = split(basis.T)
        rhs = (wide([part[0] for part in parts]), wide([part[1] for part in parts]))
        row = dot_split(turned, rhs)
        for col in range(level_no + 2):
            store(offset(level_no) + col, row[:, col * rank : (col + 1) * rank])


def eye(rank):
    shape = (rank, rank)
    row = lax.broadcasted_iota(jnp.int32, shape, 0)
    col = lax.broadcasted_iota(jnp.int32, shape, 1)
    return (row == col).astype(jnp.float32)


def square_step(inverse, power):
    rank = power.shape[0]
    both = dot3(power, wide([inverse, power]))
    return inverse + both[:, :rank], both[:, rank:]


def solve_pair(left_row, right_row, inverse_of):
    rank = left_row.shape[0]
    gram_a, gram_b = left_row[:, -rank:], right_row[:, -rank:]
    proj_a, proj_b = left_row[:, :-rank], right_row[:, :-rank]
    first = dot3(gram_a, wide([gram_b, proj_b]))
    inverse = inverse_of(first[:, :rank])
    coef_b = dot3(inverse, proj_a - first[:, rank:])
    coef_a = proj_b - dot3(gram_b, coef_b)
    return coef_a, coef_b


def adaptive_inverse(matrix):
    identity = eye(matrix.shape[0])

    def unfinished(state):
        step, _, power = state
        size = jnp.sum(power * power)
        return jnp.logical_and(size > 1e-14, step < 64)

    def body(state):
        step, inverse, power = state
        inverse, power = square_step(inverse, power)
        return step + 1, inverse, power

    state = (0, identity + matrix, dot3(matrix, matrix))
    return lax.while_loop(unfinished, body, state)[1]


def merged_rows(level_no, own, sib, sides, coef_a, coef_b, store):
    rank = coef_a.shape[0]
    proj_a, proj_b = sides[0][:, :-rank], sides[1][:, :-rank]
    stacked = jnp.concatenate([coef_a, coef_b], axis=0)
    rhs = split(jnp.concatenate([proj_a + coef_b, proj_b + coef_a], axis=0))
    for row_no in range(level_no):
        columns = slice((row_no + 1) * rank, (row_no + 2) * rank)
        turned = split(stacked[:, columns].T)
        end = (row_no + 2) * rank
        change = dot_split(turned, (rhs[0][:, :end], rhs[1][:, :end]))
        for col in range(row_no + 2):
            slot = offset(row_no) + col
            store(slot, own(slot) + sib(slot) - change[:, col * rank : (col + 1) * rank])


def final_coefs(coef_of, levels):
    deltas = []
    for level_no in range(levels):
        delta = coef_of(level_no, 0)
        if deltas:
            known = jnp.concatenate(deltas, axis=0)
            delta = delta - dot3(wide([coef_of(level_no, 1 + i) for i in range(level_no)]), known)
        deltas.append(delta)
    return deltas


def gram_kernel(bases_ref, targets_ref, out_ref):
    def store(slot, value):
        out_ref[slot] = value

    gram_rows(bases_ref, targets_ref, store)


def level_kernel(level_no, group_bits, own_ref, sib_ref, *out_refs):
    coef_ref = out_refs[0]
    is_left = lax.rem(lax.axis_index(AXIS) // 2**group_bits, 2) == 0
    base = offset(level_no)
    own_row = wide([own_ref[base + col] for col in range(level_no + 2)])
    sib_row = wide([sib_ref[base + col] for col in range(level_no + 2)])
    sides = (jnp.where(is_left, own_row, sib_row), jnp.where(is_left, sib_row, own_row))
    coef_a, coef_b = solve_pair(*sides, adaptive_inverse)
    own_coef = jnp.where(is_left, coef_a, coef_b)
    rank = coef_a.shape[0]
    for col in range(level_no + 1):
        coef_ref[col] = own_coef[:, col * rank : (col + 1) * rank]
    if level_no:
        next_ref = out_refs[1]

        def store(slot, value):
            next_ref[slot] = value

        merged_rows(
            level_no, lambda s: own_ref[s], lambda s: sib_ref[s], sides, coef_a, coef_b, store
        )


def apply_kernel(bases_ref, targets_ref, *refs):
    levels = bases_ref.shape[0]
    coefs, out_ref = refs[:-1], refs[-1]
    deltas = final_coefs(lambda level_no, col: coefs[level_no][col], levels)
    lhs = wide([bases_ref[level_no] for level_no in range(levels)])
    out_ref[...] = targets_ref[...] - dot3(lhs, jnp.concatenate(deltas, axis=0))


def call(kernel, outs, args):
    return pl.pallas_call(
        kernel,
        out_shape=outs,
        in_specs=[VMEM_SPEC] * len(args),
        out_specs=jax.tree.map(lambda _: VMEM_SPEC, outs),
        compiler_params=pltpu.CompilerParams(vmem_limit_bytes=VMEM_LIMIT),
    )(*args)


def from_partner(value, bit_no):
    pairs = [(source, source ^ 2**bit_no) for source in range(lax.axis_size(AXIS))]
    return lax.ppermute(value, AXIS, pairs)


def blocks(count, rank):
    return jax.ShapeDtypeStruct((count, rank, rank), jnp.float32)


SQUARINGS = 3
RESIDUAL = 1e-7


def fixed_inverse(matrix):
    inverse, power = eye(matrix.shape[0]) + matrix, dot3(matrix, matrix)
    for _ in range(SQUARINGS):
        inverse, power = square_step(inverse, power)
    return inverse, power


def fused_kernel(depth, bases_ref, targets_ref, out_ref, flag_ref, *refs):
    levels, _, rank = bases_ref.shape
    half = rank // 2
    sums, taken = refs[:depth], refs[depth : 2 * depth]
    coef, turned_ref, moved, flag_own, flag_in = refs[2 * depth : 2 * depth + 5]
    sems = refs[2 * depth + 5 :]
    link_send, link_recv, core_send, core_recv, relay_send, relay_recv, flag_send, flag_recv = sems
    me = lax.axis_index(AXIS)
    core = lax.rem(me, 2)
    own_half = pl.ds(pl.multiple_of(core * half, half), half)
    other_half = pl.ds(pl.multiple_of((1 - core) * half, half), half)
    pending = []

    def side(bit):
        return lax.rem(me // 2**bit, 2)

    def partner(bit):
        return me + 2**bit * (1 - 2 * side(bit))

    def push(src, dst, send, recv, bit):
        copy = pltpu.make_async_remote_copy(
            src_ref=src,
            dst_ref=dst,
            send_sem=send,
            recv_sem=recv,
            device_id=(partner(bit),),
            device_id_type=pl.DeviceIdType.MESH,
        )
        copy.start()
        pending.append(copy)
        return copy

    barrier = pltpu.get_barrier_semaphore()
    for bit in range(depth):
        pl.semaphore_signal(
            barrier, inc=1, device_id=(partner(bit),), device_id_type=pl.DeviceIdType.MESH
        )

    links, swaps = {}, {}

    def send_row(bit, row):
        slots = pl.ds(offset(row), row + 2)
        critical = row == depth - 1 - bit
        if bit == 0:
            region = (slots,) if critical else (slots, other_half)
        else:
            region = (slots, own_half)
        src, dst = sums[bit].at[region], taken[bit].at[region]
        links[bit, row] = push(src, dst, link_send.at[bit, row], link_recv.at[bit, row], bit)
        if critical and bit:
            swaps[bit] = push(src, src, core_send.at[bit], core_recv.at[bit], 0)

    def begin(bit, row):
        if (bit, row) not in links:
            send_row(bit, row)

    def settle(bit, row):
        copy = links[bit, row]
        if bit and any(copy is other for other in pending):
            copy.wait_send()
            pending[:] = [other for other in pending if other is not copy]

    parts = [split(targets_ref[...])] + [split(bases_ref[i]) for i in range(levels)]
    high, low = wide([part[0] for part in parts]), wide([part[1] for part in parts])
    for row in reversed(range(levels)):
        end = (row + 2) * rank
        value = dot_split(split(bases_ref[row].T), (high[:, :end], low[:, :end]))
        for col in range(row + 2):
            sums[0][offset(row) + col] = value[:, col * rank : (col + 1) * rank]
        if row == levels - 1:
            pl.semaphore_wait(barrier, depth)
        send_row(0, row)

    def coef_slot(level_no, col):
        return level_no * (level_no + 1) // 2 + col

    def move_rows():
        deltas = []
        for level_no in range(1, levels):
            delta = wide([coef[coef_slot(level_no, col)] for col in range(2)])
            if deltas:
                lhs = wide([coef[coef_slot(level_no, 1 + i)] for i in range(1, level_no)])
                delta = delta - dot3(lhs, jnp.concatenate(deltas, axis=0))
            deltas.append(delta)
        change = dot_split((high[:, 2 * rank :], low[:, 2 * rank :]), split(jnp.concatenate(deltas, axis=0)))
        moved[:, :rank] = targets_ref[...] - change[:, :rank]
        moved[:, rank:] = bases_ref[0] - change[:, rank:]

    def merge_row(bit, row, change_of):
        links[bit, row].wait_recv()
        change = change_of(row)
        for col in range(row + 2):
            slot = offset(row) + col
            value = sums[bit][slot, own_half, :] + taken[bit][slot, own_half, :]
            if change is not None:
                value = value - change[:, col * rank : (col + 1) * rank]
            sums[bit + 1][slot, own_half, :] = value

    def changes(coef_a, coef_b, left_row, right_row):
        proj_a, proj_b = left_row[:, :-rank], right_row[:, :-rank]
        stacked = jnp.concatenate([coef_a, coef_b], axis=0)
        rhs = split(jnp.concatenate([proj_a + coef_b, proj_b + coef_a], axis=0))

        def change_of(row):
            turned_ref[...] = stacked[:, (row + 1) * rank : (row + 2) * rank].T
            end = (row + 2) * rank
            return dot_split(split(turned_ref[own_half, :]), (rhs[0][:, :end], rhs[1][:, :end]))

        return change_of

    flag = jnp.zeros((8, 128), jnp.float32)
    late, late_change = [], None
    for bit in range(depth):
        level_no = depth - 1 - bit
        solving = level_no < levels
        rest = list(reversed(range(min(level_no, levels))))
        if bit:
            flag_own[bit] = flag
            flag_copy = push(
                flag_own.at[bit], flag_in.at[bit], flag_send.at[bit], flag_recv.at[bit], bit
            )
        if level_no == 0:
            move_rows()
        change_of = lambda row: None
        if solving:
            for place, row in enumerate(late):
                settle(bit - 1, row)
                if place + 1 < len(late):
                    begin(bit - 1, late[place + 1])
                merge_row(bit - 1, row, late_change)
                if row == rest[0]:
                    settle(bit, level_no)
                    begin(bit, row)
            slots = pl.ds(offset(level_no), level_no + 2)
            links[bit, level_no].wait_recv()
            if bit:
                region = taken[bit].at[slots, own_half]
                relay = push(region, region, relay_send.at[bit], relay_recv.at[bit], 0)
            if bit:
                swaps[bit].wait_recv()
                relay.wait_recv()
            base = offset(level_no)
            own_row = wide([sums[bit][base + col] for col in range(level_no + 2)])
            sib_row = wide([taken[bit][base + col] for col in range(level_no + 2)])
            is_left = side(bit) == 0
            left_row = jnp.where(is_left, own_row, sib_row)
            right_row = jnp.where(is_left, sib_row, own_row)
            state = []

            def inverse_of(matrix):
                inverse, power = fixed_inverse(matrix)
                state.append(jnp.max((power * power).reshape(rank // 8, 8, rank), axis=0))
                return inverse

            coef_a, coef_b = solve_pair(left_row, right_row, inverse_of)
            flag = jnp.maximum(flag, state[0])
            own_coef = jnp.where(is_left, coef_a, coef_b)
            for col in range(level_no + 1):
                coef[coef_slot(level_no, col)] = own_coef[:, col * rank : (col + 1) * rank]
            if level_no == 0:
                out_ref[...] = moved[:, :rank] - dot3(moved[:, rank:], own_coef)
            else:
                change_of = changes(coef_a, coef_b, left_row, right_row)
        if rest:
            following = level_no - 1 < levels
            late = rest[1:] if following else []
            late_change = change_of
            if late:
                settle(bit, rest[0])
                begin(bit, late[0])
            for row in rest[:1] if following else rest:
                merge_row(bit, row, change_of)
                begin(bit + 1, row)
        if bit:
            flag_copy.wait_recv()
            flag = jnp.maximum(flag, flag_in[bit])
    flag_ref[...] = flag
    for copy in pending:
        copy.wait_send()


def fused(bases, targets, depth):
    levels, rows, rank = bases.shape
    stages = [
        pltpu.VMEM((offset(min(depth - bit, levels)), rank, rank), jnp.float32)
        for bit in range(depth)
    ]
    dma = pltpu.SemaphoreType.DMA
    return pl.pallas_call(
        functools.partial(fused_kernel, depth),
        out_shape=(
            jax.ShapeDtypeStruct(targets.shape, jnp.float32),
            jax.ShapeDtypeStruct((8, 128), jnp.float32),
        ),
        in_specs=[VMEM_SPEC] * 2,
        out_specs=(VMEM_SPEC,) * 2,
        scratch_shapes=stages
        + stages
        + [
            pltpu.VMEM((levels * (levels + 1) // 2, rank, rank), jnp.float32),
            pltpu.VMEM((rank, 2 * rank), jnp.float32),
            pltpu.VMEM((rows, 2 * rank), jnp.float32),
            pltpu.VMEM((depth, 8, 128), jnp.float32),
            pltpu.VMEM((depth, 8, 128), jnp.float32),
        ]
        + [dma((depth, levels))] * 2
        + [dma((depth,))] * 6,
        compiler_params=pltpu.CompilerParams(
            collective_id=0, has_side_effects=True, vmem_limit_bytes=VMEM_LIMIT
        ),
    )(bases, targets)


def general(bases, targets):
    levels, _, rank = bases.shape
    tree_depth = lax.axis_size(AXIS).bit_length() - 1
    sums = call(gram_kernel, blocks(offset(levels), rank), (bases, targets))
    for bit_no in range(tree_depth - levels):
        sums = sums + from_partner(sums, bit_no)
    coefs = [None] * levels
    for level_no in reversed(range(levels)):
        group_bits = tree_depth - level_no - 1
        sibling = from_partner(sums, group_bits)
        outs = [blocks(level_no + 1, rank)]
        if level_no:
            outs.append(blocks(offset(level_no), rank))
        kernel = functools.partial(level_kernel, level_no, group_bits)
        coefs[level_no], *rest = call(kernel, tuple(outs), (sums, sibling))
        sums = rest[0] if rest else None
    out = jax.ShapeDtypeStruct(targets.shape, jnp.float32)
    return call(apply_kernel, out, (bases, targets, *coefs))


def per_device(bases, targets):
    depth = lax.axis_size(AXIS).bit_length() - 1
    out, residual = fused(bases, targets, depth)
    limit = (RESIDUAL / bases.shape[2]) ** 2
    return lax.cond(
        jnp.max(residual) < limit, lambda b, t, o: o, lambda b, t, o: general(b, t), bases, targets, out
    )


def solution(mesh):
    return jax.shard_map(
        per_device,
        mesh=mesh,
        in_specs=(P(None, AXIS, None), P(AXIS, None)),
        out_specs=P(AXIS, None),
        check_vma=False,
    )
```

```python
import functools

import jax
import jax.numpy as jnp
from jax import lax
from jax.experimental import pallas as pl
from jax.experimental.pallas import tpu as pltpu
from jax.sharding import PartitionSpec as P

AXIS = "rows"
VMEM_LIMIT = 48 * 2**20
FUSED_LIMIT = 62 * 2**20
VMEM_SPEC = pl.BlockSpec(memory_space=pltpu.VMEM)


def offset(level_no):
    return level_no * (level_no + 3) // 2


def split(value):
    high = value.astype(jnp.bfloat16)
    low = (value - high.astype(jnp.float32)).astype(jnp.bfloat16)
    return high, low


def dot_split(left, right):
    left_high, left_low = left
    right_high, right_low = right
    dot = functools.partial(jnp.dot, preferred_element_type=jnp.float32)
    return (dot(left_low, right_high) + dot(left_high, right_low)) + dot(left_high, right_high)


def dot3(left, right):
    return dot_split(split(left), split(right))


def wide(blocks):
    return jnp.concatenate(blocks, axis=1)


def gram_rows(bases_ref, targets_ref, store):
    levels = bases_ref.shape[0]
    rank = bases_ref.shape[2]
    parts = [split(targets_ref[...])]
    for level_no in range(levels):
        basis = bases_ref[level_no]
        parts.append(split(basis))
        turned = split(basis.T)
        rhs = (wide([part[0] for part in parts]), wide([part[1] for part in parts]))
        row = dot_split(turned, rhs)
        for col in range(level_no + 2):
            store(offset(level_no) + col, row[:, col * rank : (col + 1) * rank])


def eye(rank):
    shape = (rank, rank)
    row = lax.broadcasted_iota(jnp.int32, shape, 0)
    col = lax.broadcasted_iota(jnp.int32, shape, 1)
    return (row == col).astype(jnp.float32)


def square_step(inverse, power):
    rank = power.shape[0]
    both = dot3(power, wide([inverse, power]))
    return inverse + both[:, :rank], both[:, rank:]


def solve_pair(left_row, right_row, inverse_of):
    rank = left_row.shape[0]
    gram_a, gram_b = left_row[:, -rank:], right_row[:, -rank:]
    proj_a, proj_b = left_row[:, :-rank], right_row[:, :-rank]
    first = dot3(gram_a, wide([gram_b, proj_b]))
    inverse = inverse_of(first[:, :rank])
    coef_b = dot3(inverse, proj_a - first[:, rank:])
    coef_a = proj_b - dot3(gram_b, coef_b)
    return coef_a, coef_b


def adaptive_inverse(matrix):
    identity = eye(matrix.shape[0])

    def unfinished(state):
        step, _, power = state
        size = jnp.sum(power * power)
        return jnp.logical_and(size > 1e-14, step < 64)

    def body(state):
        step, inverse, power = state
        inverse, power = square_step(inverse, power)
        return step + 1, inverse, power

    state = (0, identity + matrix, dot3(matrix, matrix))
    return lax.while_loop(unfinished, body, state)[1]


def merged_rows(level_no, own, sib, sides, coef_a, coef_b, store):
    rank = coef_a.shape[0]
    proj_a, proj_b = sides[0][:, :-rank], sides[1][:, :-rank]
    stacked = jnp.concatenate([coef_a, coef_b], axis=0)
    rhs = split(jnp.concatenate([proj_a + coef_b, proj_b + coef_a], axis=0))
    for row_no in range(level_no):
        columns = slice((row_no + 1) * rank, (row_no + 2) * rank)
        turned = split(stacked[:, columns].T)
        end = (row_no + 2) * rank
        change = dot_split(turned, (rhs[0][:, :end], rhs[1][:, :end]))
        for col in range(row_no + 2):
            slot = offset(row_no) + col
            store(slot, own(slot) + sib(slot) - change[:, col * rank : (col + 1) * rank])


def final_coefs(coef_of, levels):
    deltas = []
    for level_no in range(levels):
        delta = coef_of(level_no, 0)
        if deltas:
            known = jnp.concatenate(deltas, axis=0)
            delta = delta - dot3(wide([coef_of(level_no, 1 + i) for i in range(level_no)]), known)
        deltas.append(delta)
    return deltas


def gram_kernel(bases_ref, targets_ref, out_ref):
    def store(slot, value):
        out_ref[slot] = value

    gram_rows(bases_ref, targets_ref, store)


def level_kernel(level_no, group_bits, own_ref, sib_ref, *out_refs):
    coef_ref = out_refs[0]
    is_left = lax.rem(lax.axis_index(AXIS) // 2**group_bits, 2) == 0
    base = offset(level_no)
    own_row = wide([own_ref[base + col] for col in range(level_no + 2)])
    sib_row = wide([sib_ref[base + col] for col in range(level_no + 2)])
    sides = (jnp.where(is_left, own_row, sib_row), jnp.where(is_left, sib_row, own_row))
    coef_a, coef_b = solve_pair(*sides, adaptive_inverse)
    own_coef = jnp.where(is_left, coef_a, coef_b)
    rank = coef_a.shape[0]
    for col in range(level_no + 1):
        coef_ref[col] = own_coef[:, col * rank : (col + 1) * rank]
    if level_no:
        next_ref = out_refs[1]

        def store(slot, value):
            next_ref[slot] = value

        merged_rows(
            level_no, lambda s: own_ref[s], lambda s: sib_ref[s], sides, coef_a, coef_b, store
        )


def apply_kernel(bases_ref, targets_ref, *refs):
    levels = bases_ref.shape[0]
    coefs, out_ref = refs[:-1], refs[-1]
    deltas = final_coefs(lambda level_no, col: coefs[level_no][col], levels)
    lhs = wide([bases_ref[level_no] for level_no in range(levels)])
    out_ref[...] = targets_ref[...] - dot3(lhs, jnp.concatenate(deltas, axis=0))


def call(kernel, outs, args):
    return pl.pallas_call(
        kernel,
        out_shape=outs,
        in_specs=[VMEM_SPEC] * len(args),
        out_specs=jax.tree.map(lambda _: VMEM_SPEC, outs),
        compiler_params=pltpu.CompilerParams(vmem_limit_bytes=VMEM_LIMIT),
    )(*args)


def from_partner(value, bit_no):
    pairs = [(source, source ^ 2**bit_no) for source in range(lax.axis_size(AXIS))]
    return lax.ppermute(value, AXIS, pairs)


def blocks(count, rank):
    return jax.ShapeDtypeStruct((count, rank, rank), jnp.float32)


SQUARINGS = 3
RESIDUAL = 1e-7


def fixed_inverse(matrix):
    inverse, power = eye(matrix.shape[0]) + matrix, dot3(matrix, matrix)
    for _ in range(SQUARINGS):
        inverse, power = square_step(inverse, power)
    return inverse, power


def fused_kernel(depth, bases_in, targets_in, out_ref, flag_ref, *refs):
    levels, _, rank = bases_in.shape
    half = rank // 2
    sums, taken = refs[:depth], refs[depth : 2 * depth]
    coef, turned_ref, moved, flag_own, flag_in = refs[2 * depth : 2 * depth + 5]
    bases_ref, targets_ref, load = refs[2 * depth + 5 : 2 * depth + 8]
    sems = refs[2 * depth + 8 :]
    loads = [pltpu.make_async_copy(targets_in, targets_ref, load.at[levels])]
    for level_no in range(levels):
        loads.append(
            pltpu.make_async_copy(
                bases_in.at[level_no], bases_ref.at[level_no], load.at[level_no]
            )
        )
    for copy in loads:
        copy.start()
    link_send, link_recv, core_send, core_recv, relay_send, relay_recv, flag_send, flag_recv = sems
    me = lax.axis_index(AXIS)
    core = lax.rem(me, 2)
    own_half = pl.ds(pl.multiple_of(core * half, half), half)
    other_half = pl.ds(pl.multiple_of((1 - core) * half, half), half)
    pending = []

    def side(bit):
        return lax.rem(me // 2**bit, 2)

    def partner(bit):
        return me + 2**bit * (1 - 2 * side(bit))

    def push(src, dst, send, recv, bit):
        copy = pltpu.make_async_remote_copy(
            src_ref=src,
            dst_ref=dst,
            send_sem=send,
            recv_sem=recv,
            device_id=(partner(bit),),
            device_id_type=pl.DeviceIdType.MESH,
        )
        copy.start()
        pending.append(copy)
        return copy

    barrier = pltpu.get_barrier_semaphore()
    for bit in range(depth):
        pl.semaphore_signal(
            barrier, inc=1, device_id=(partner(bit),), device_id_type=pl.DeviceIdType.MESH
        )

    links, swaps = {}, {}

    def send_row(bit, row):
        slots = pl.ds(offset(row), row + 2)
        critical = row == depth - 1 - bit
        if bit == 0:
            region = (slots,) if critical else (slots, other_half)
        else:
            region = (slots, own_half)
        src, dst = sums[bit].at[region], taken[bit].at[region]
        links[bit, row] = push(src, dst, link_send.at[bit, row], link_recv.at[bit, row], bit)
        if critical and bit:
            swaps[bit] = push(src, src, core_send.at[bit], core_recv.at[bit], 0)

    def begin(bit, row):
        if (bit, row) not in links:
            send_row(bit, row)

    parts = []
    for place, copy in enumerate(loads):
        copy.wait()
        parts.append(split(bases_ref[place - 1] if place else targets_ref[...]))
    high, low = wide([part[0] for part in parts]), wide([part[1] for part in parts])
    for row in reversed(range(levels)):
        end = (row + 2) * rank
        value = dot_split(split(bases_ref[row].T), (high[:, :end], low[:, :end]))
        for col in range(row + 2):
            sums[0][offset(row) + col] = value[:, col * rank : (col + 1) * rank]
        if row == levels - 1:
            pl.semaphore_wait(barrier, depth)
        send_row(0, row)

    def coef_slot(level_no, col):
        return level_no * (level_no + 1) // 2 + col

    def move_rows():
        deltas = []
        for level_no in range(1, levels):
            delta = wide([coef[coef_slot(level_no, col)] for col in range(2)])
            if deltas:
                lhs = wide([coef[coef_slot(level_no, 1 + i)] for i in range(1, level_no)])
                delta = delta - dot3(lhs, jnp.concatenate(deltas, axis=0))
            deltas.append(delta)
        change = dot_split((high[:, 2 * rank :], low[:, 2 * rank :]), split(jnp.concatenate(deltas, axis=0)))
        moved[:, :rank] = targets_ref[...] - change[:, :rank]
        moved[:, rank:] = bases_ref[0] - change[:, rank:]

    def merge_row(bit, row, change_of):
        links[bit, row].wait_recv()
        change = change_of(row)
        for col in range(row + 2):
            slot = offset(row) + col
            value = sums[bit][slot, own_half, :] + taken[bit][slot, own_half, :]
            if change is not None:
                value = value - change[:, col * rank : (col + 1) * rank]
            sums[bit + 1][slot, own_half, :] = value

    def changes(coef_a, coef_b, left_row, right_row):
        proj_a, proj_b = left_row[:, :-rank], right_row[:, :-rank]
        stacked = jnp.concatenate([coef_a, coef_b], axis=0)
        rhs = split(jnp.concatenate([proj_a + coef_b, proj_b + coef_a], axis=0))

        def change_of(row):
            turned_ref[...] = stacked[:, (row + 1) * rank : (row + 2) * rank].T
            end = (row + 2) * rank
            return dot_split(split(turned_ref[own_half, :]), (rhs[0][:, :end], rhs[1][:, :end]))

        return change_of

    flag = jnp.zeros((8, 128), jnp.float32)
    late, late_change = [], None
    for bit in range(depth):
        level_no = depth - 1 - bit
        solving = level_no < levels
        rest = list(reversed(range(min(level_no, levels))))
        if bit:
            flag_own[bit] = flag
            flag_copy = push(
                flag_own.at[bit], flag_in.at[bit], flag_send.at[bit], flag_recv.at[bit], bit
            )
        if level_no == 0:
            move_rows()
        change_of = lambda row: None
        if solving:
            for row in late:
                merge_row(bit - 1, row, late_change)
            slots = pl.ds(offset(level_no), level_no + 2)
            links[bit, level_no].wait_recv()
            if bit:
                region = taken[bit].at[slots, own_half]
                relay = push(region, region, relay_send.at[bit], relay_recv.at[bit], 0)
            for row in rest:
                begin(bit, row)
            if bit:
                swaps[bit].wait_recv()
                relay.wait_recv()
            base = offset(level_no)
            own_row = wide([sums[bit][base + col] for col in range(level_no + 2)])
            sib_row = wide([taken[bit][base + col] for col in range(level_no + 2)])
            is_left = side(bit) == 0
            left_row = jnp.where(is_left, own_row, sib_row)
            right_row = jnp.where(is_left, sib_row, own_row)
            state = []

            def inverse_of(matrix):
                inverse, power = fixed_inverse(matrix)
                state.append(jnp.max((power * power).reshape(rank // 8, 8, rank), axis=0))
                return inverse

            coef_a, coef_b = solve_pair(left_row, right_row, inverse_of)
            flag = jnp.maximum(flag, state[0])
            own_coef = jnp.where(is_left, coef_a, coef_b)
            for col in range(level_no + 1):
                coef[coef_slot(level_no, col)] = own_coef[:, col * rank : (col + 1) * rank]
            if level_no == 0:
                out_ref[...] = moved[:, :rank] - dot3(moved[:, rank:], own_coef)
            else:
                change_of = changes(coef_a, coef_b, left_row, right_row)
        if rest:
            following = level_no - 1 < levels
            late = rest[1:] if following else []
            late_change = change_of
            for row in rest[:1] if following else rest:
                merge_row(bit, row, change_of)
                begin(bit + 1, row)
        if bit:
            flag_copy.wait_recv()
            flag = jnp.maximum(flag, flag_in[bit])
    flag_ref[...] = flag
    for copy in pending:
        copy.wait_send()


def fused(bases, targets, depth):
    levels, rows, rank = bases.shape
    stages = [
        pltpu.VMEM((offset(min(depth - bit, levels)), rank, rank), jnp.float32)
        for bit in range(depth)
    ]
    dma = pltpu.SemaphoreType.DMA
    return pl.pallas_call(
        functools.partial(fused_kernel, depth),
        out_shape=(
            jax.ShapeDtypeStruct(targets.shape, jnp.float32),
            jax.ShapeDtypeStruct((8, 128), jnp.float32),
        ),
        in_specs=[pl.BlockSpec(memory_space=pl.ANY)] * 2,
        out_specs=(VMEM_SPEC,) * 2,
        scratch_shapes=stages
        + stages
        + [
            pltpu.VMEM((levels * (levels + 1) // 2, rank, rank), jnp.float32),
            pltpu.VMEM((rank, 2 * rank), jnp.float32),
            pltpu.VMEM((rows, 2 * rank), jnp.float32),
            pltpu.VMEM((depth, 8, 128), jnp.float32),
            pltpu.VMEM((depth, 8, 128), jnp.float32),
            pltpu.VMEM(bases.shape, jnp.float32),
            pltpu.VMEM(targets.shape, jnp.float32),
            dma((levels + 1,)),
        ]
        + [dma((depth, levels))] * 2
        + [dma((depth,))] * 6,
        compiler_params=pltpu.CompilerParams(
            collective_id=0, has_side_effects=True, vmem_limit_bytes=FUSED_LIMIT
        ),
    )(bases, targets)


def general(bases, targets):
    levels, _, rank = bases.shape
    tree_depth = lax.axis_size(AXIS).bit_length() - 1
    sums = call(gram_kernel, blocks(offset(levels), rank), (bases, targets))
    for bit_no in range(tree_depth - levels):
        sums = sums + from_partner(sums, bit_no)
    coefs = [None] * levels
    for level_no in reversed(range(levels)):
        group_bits = tree_depth - level_no - 1
        sibling = from_partner(sums, group_bits)
        outs = [blocks(level_no + 1, rank)]
        if level_no:
            outs.append(blocks(offset(level_no), rank))
        kernel = functools.partial(level_kernel, level_no, group_bits)
        coefs[level_no], *rest = call(kernel, tuple(outs), (sums, sibling))
        sums = rest[0] if rest else None
    out = jax.ShapeDtypeStruct(targets.shape, jnp.float32)
    return call(apply_kernel, out, (bases, targets, *coefs))


def per_device(bases, targets):
    depth = lax.axis_size(AXIS).bit_length() - 1
    out, residual = fused(bases, targets, depth)
    limit = (RESIDUAL / bases.shape[2]) ** 2
    return lax.cond(
        jnp.max(residual) < limit, lambda b, t, o: o, lambda b, t, o: general(b, t), bases, targets, out
    )


def solution(mesh):
    return jax.shard_map(
        per_device,
        mesh=mesh,
        in_specs=(P(None, AXIS, None), P(AXIS, None)),
        out_specs=P(AXIS, None),
        check_vma=False,
    )
```

```python
import functools

import jax
import jax.numpy as jnp
from jax import lax
from jax.experimental import pallas as pl
from jax.experimental.pallas import tpu as pltpu
from jax.sharding import PartitionSpec as P

AXIS = "rows"
VMEM_LIMIT = 48 * 2**20
FUSED_LIMIT = 62 * 2**20
VMEM_SPEC = pl.BlockSpec(memory_space=pltpu.VMEM)


def offset(level_no):
    return level_no * (level_no + 3) // 2


def split(value):
    high = value.astype(jnp.bfloat16)
    low = (value - high.astype(jnp.float32)).astype(jnp.bfloat16)
    return high, low


def dot_split(left, right):
    left_high, left_low = left
    right_high, right_low = right
    dot = functools.partial(jnp.dot, preferred_element_type=jnp.float32)
    return (dot(left_low, right_high) + dot(left_high, right_low)) + dot(left_high, right_high)


def dot3(left, right):
    return dot_split(split(left), split(right))


def wide(blocks):
    return jnp.concatenate(blocks, axis=1)


def gram_rows(bases_ref, targets_ref, store):
    levels = bases_ref.shape[0]
    rank = bases_ref.shape[2]
    parts = [split(targets_ref[...])]
    for level_no in range(levels):
        basis = bases_ref[level_no]
        parts.append(split(basis))
        turned = split(basis.T)
        rhs = (wide([part[0] for part in parts]), wide([part[1] for part in parts]))
        row = dot_split(turned, rhs)
        for col in range(level_no + 2):
            store(offset(level_no) + col, row[:, col * rank : (col + 1) * rank])


def eye(rank):
    shape = (rank, rank)
    row = lax.broadcasted_iota(jnp.int32, shape, 0)
    col = lax.broadcasted_iota(jnp.int32, shape, 1)
    return (row == col).astype(jnp.float32)


def square_step(inverse, power):
    rank = power.shape[0]
    both = dot3(power, wide([inverse, power]))
    return inverse + both[:, :rank], both[:, rank:]


def solve_pair(left_row, right_row, inverse_of):
    rank = left_row.shape[0]
    gram_a, gram_b = left_row[:, -rank:], right_row[:, -rank:]
    proj_a, proj_b = left_row[:, :-rank], right_row[:, :-rank]
    first = dot3(gram_a, wide([gram_b, proj_b]))
    inverse = inverse_of(first[:, :rank])
    coef_b = dot3(inverse, proj_a - first[:, rank:])
    coef_a = proj_b - dot3(gram_b, coef_b)
    return coef_a, coef_b


def adaptive_inverse(matrix):
    identity = eye(matrix.shape[0])

    def unfinished(state):
        step, _, power = state
        size = jnp.sum(power * power)
        return jnp.logical_and(size > 1e-14, step < 64)

    def body(state):
        step, inverse, power = state
        inverse, power = square_step(inverse, power)
        return step + 1, inverse, power

    state = (0, identity + matrix, dot3(matrix, matrix))
    return lax.while_loop(unfinished, body, state)[1]


def merged_rows(level_no, own, sib, sides, coef_a, coef_b, store):
    rank = coef_a.shape[0]
    proj_a, proj_b = sides[0][:, :-rank], sides[1][:, :-rank]
    stacked = jnp.concatenate([coef_a, coef_b], axis=0)
    rhs = split(jnp.concatenate([proj_a + coef_b, proj_b + coef_a], axis=0))
    for row_no in range(level_no):
        columns = slice((row_no + 1) * rank, (row_no + 2) * rank)
        turned = split(stacked[:, columns].T)
        end = (row_no + 2) * rank
        change = dot_split(turned, (rhs[0][:, :end], rhs[1][:, :end]))
        for col in range(row_no + 2):
            slot = offset(row_no) + col
            store(slot, own(slot) + sib(slot) - change[:, col * rank : (col + 1) * rank])


def final_coefs(coef_of, levels):
    deltas = []
    for level_no in range(levels):
        delta = coef_of(level_no, 0)
        if deltas:
            known = jnp.concatenate(deltas, axis=0)
            delta = delta - dot3(wide([coef_of(level_no, 1 + i) for i in range(level_no)]), known)
        deltas.append(delta)
    return deltas


def gram_kernel(bases_ref, targets_ref, out_ref):
    def store(slot, value):
        out_ref[slot] = value

    gram_rows(bases_ref, targets_ref, store)


def level_kernel(level_no, group_bits, own_ref, sib_ref, *out_refs):
    coef_ref = out_refs[0]
    is_left = lax.rem(lax.axis_index(AXIS) // 2**group_bits, 2) == 0
    base = offset(level_no)
    own_row = wide([own_ref[base + col] for col in range(level_no + 2)])
    sib_row = wide([sib_ref[base + col] for col in range(level_no + 2)])
    sides = (jnp.where(is_left, own_row, sib_row), jnp.where(is_left, sib_row, own_row))
    coef_a, coef_b = solve_pair(*sides, adaptive_inverse)
    own_coef = jnp.where(is_left, coef_a, coef_b)
    rank = coef_a.shape[0]
    for col in range(level_no + 1):
        coef_ref[col] = own_coef[:, col * rank : (col + 1) * rank]
    if level_no:
        next_ref = out_refs[1]

        def store(slot, value):
            next_ref[slot] = value

        merged_rows(
            level_no, lambda s: own_ref[s], lambda s: sib_ref[s], sides, coef_a, coef_b, store
        )


def apply_kernel(bases_ref, targets_ref, *refs):
    levels = bases_ref.shape[0]
    coefs, out_ref = refs[:-1], refs[-1]
    deltas = final_coefs(lambda level_no, col: coefs[level_no][col], levels)
    lhs = wide([bases_ref[level_no] for level_no in range(levels)])
    out_ref[...] = targets_ref[...] - dot3(lhs, jnp.concatenate(deltas, axis=0))


def call(kernel, outs, args):
    return pl.pallas_call(
        kernel,
        out_shape=outs,
        in_specs=[VMEM_SPEC] * len(args),
        out_specs=jax.tree.map(lambda _: VMEM_SPEC, outs),
        compiler_params=pltpu.CompilerParams(vmem_limit_bytes=VMEM_LIMIT),
    )(*args)


def from_partner(value, bit_no):
    pairs = [(source, source ^ 2**bit_no) for source in range(lax.axis_size(AXIS))]
    return lax.ppermute(value, AXIS, pairs)


def blocks(count, rank):
    return jax.ShapeDtypeStruct((count, rank, rank), jnp.float32)


SQUARINGS = 3
RESIDUAL = 1e-7


def fixed_inverse(matrix):
    inverse, power = eye(matrix.shape[0]) + matrix, dot3(matrix, matrix)
    for _ in range(SQUARINGS):
        inverse, power = square_step(inverse, power)
    return inverse, power


def fused_kernel(depth, bases_in, targets_in, out_ref, flag_ref, *refs):
    levels, _, rank = bases_in.shape
    half = rank // 2
    sums, taken = refs[:depth], refs[depth : 2 * depth]
    coef, turned_ref, moved, flag_own, flag_in = refs[2 * depth : 2 * depth + 5]
    bases_ref, targets_ref, load = refs[2 * depth + 5 : 2 * depth + 8]
    sems = refs[2 * depth + 8 :]
    loads = [pltpu.make_async_copy(targets_in, targets_ref, load.at[levels])]
    for level_no in range(levels):
        loads.append(
            pltpu.make_async_copy(
                bases_in.at[level_no], bases_ref.at[level_no], load.at[level_no]
            )
        )
    for copy in loads:
        copy.start()
    link_send, link_recv, core_send, core_recv, relay_send, relay_recv, flag_send, flag_recv = sems
    me = lax.axis_index(AXIS)
    core = lax.rem(me, 2)
    own_half = pl.ds(pl.multiple_of(core * half, half), half)
    other_half = pl.ds(pl.multiple_of((1 - core) * half, half), half)
    pending = []

    def side(bit):
        return lax.rem(me // 2**bit, 2)

    def partner(bit):
        return me + 2**bit * (1 - 2 * side(bit))

    def push(src, dst, send, recv, bit):
        copy = pltpu.make_async_remote_copy(
            src_ref=src,
            dst_ref=dst,
            send_sem=send,
            recv_sem=recv,
            device_id=(partner(bit),),
            device_id_type=pl.DeviceIdType.MESH,
        )
        copy.start()
        pending.append(copy)
        return copy

    barrier = pltpu.get_barrier_semaphore()
    for bit in range(depth):
        pl.semaphore_signal(
            barrier, inc=1, device_id=(partner(bit),), device_id_type=pl.DeviceIdType.MESH
        )

    links, swaps = {}, {}

    def send_row(bit, row):
        slots = pl.ds(offset(row), row + 2)
        critical = row == depth - 1 - bit
        if bit == 0:
            region = (slots,) if critical else (slots, other_half)
        else:
            region = (slots, own_half)
        src, dst = sums[bit].at[region], taken[bit].at[region]
        links[bit, row] = push(src, dst, link_send.at[bit, row], link_recv.at[bit, row], bit)
        if critical and bit:
            swaps[bit] = push(src, src, core_send.at[bit], core_recv.at[bit], 0)

    def begin(bit, row):
        if (bit, row) not in links:
            send_row(bit, row)

    def settle(bit, row):
        copy = links[bit, row]
        if bit and any(copy is other for other in pending):
            copy.wait_send()
            pending[:] = [other for other in pending if other is not copy]

    parts = []
    for place, copy in enumerate(loads):
        copy.wait()
        parts.append(split(bases_ref[place - 1] if place else targets_ref[...]))
    high, low = wide([part[0] for part in parts]), wide([part[1] for part in parts])
    for row in reversed(range(levels)):
        end = (row + 2) * rank
        value = dot_split(split(bases_ref[row].T), (high[:, :end], low[:, :end]))
        for col in range(row + 2):
            sums[0][offset(row) + col] = value[:, col * rank : (col + 1) * rank]
        if row == levels - 1:
            pl.semaphore_wait(barrier, depth)
        send_row(0, row)

    def coef_slot(level_no, col):
        return level_no * (level_no + 1) // 2 + col

    def move_rows():
        deltas = []
        for level_no in range(1, levels):
            delta = wide([coef[coef_slot(level_no, col)] for col in range(2)])
            if deltas:
                lhs = wide([coef[coef_slot(level_no, 1 + i)] for i in range(1, level_no)])
                delta = delta - dot3(lhs, jnp.concatenate(deltas, axis=0))
            deltas.append(delta)
        change = dot_split((high[:, 2 * rank :], low[:, 2 * rank :]), split(jnp.concatenate(deltas, axis=0)))
        moved[:, :rank] = targets_ref[...] - change[:, :rank]
        moved[:, rank:] = bases_ref[0] - change[:, rank:]

    def merge_row(bit, row, change_of):
        links[bit, row].wait_recv()
        change = change_of(row)
        for col in range(row + 2):
            slot = offset(row) + col
            value = sums[bit][slot, own_half, :] + taken[bit][slot, own_half, :]
            if change is not None:
                value = value - change[:, col * rank : (col + 1) * rank]
            sums[bit + 1][slot, own_half, :] = value

    def changes(coef_a, coef_b, left_row, right_row):
        proj_a, proj_b = left_row[:, :-rank], right_row[:, :-rank]
        stacked = jnp.concatenate([coef_a, coef_b], axis=0)
        rhs = split(jnp.concatenate([proj_a + coef_b, proj_b + coef_a], axis=0))

        def change_of(row):
            turned_ref[...] = stacked[:, (row + 1) * rank : (row + 2) * rank].T
            end = (row + 2) * rank
            return dot_split(split(turned_ref[own_half, :]), (rhs[0][:, :end], rhs[1][:, :end]))

        return change_of

    flag = jnp.zeros((8, 128), jnp.float32)
    late, late_change = [], None
    for bit in range(depth):
        level_no = depth - 1 - bit
        solving = level_no < levels
        rest = list(reversed(range(min(level_no, levels))))
        if bit:
            flag_own[bit] = flag
            flag_copy = push(
                flag_own.at[bit], flag_in.at[bit], flag_send.at[bit], flag_recv.at[bit], bit
            )
        if level_no == 0:
            move_rows()
        change_of = lambda row: None
        if solving:
            for place, row in enumerate(late):
                settle(bit - 1, row)
                if place + 1 < len(late):
                    begin(bit - 1, late[place + 1])
                merge_row(bit - 1, row, late_change)
                if row == rest[0]:
                    settle(bit, level_no)
                    begin(bit, row)
            slots = pl.ds(offset(level_no), level_no + 2)
            links[bit, level_no].wait_recv()
            if bit:
                region = taken[bit].at[slots, own_half]
                relay = push(region, region, relay_send.at[bit], relay_recv.at[bit], 0)
            if bit:
                swaps[bit].wait_recv()
                relay.wait_recv()
            base = offset(level_no)
            own_row = wide([sums[bit][base + col] for col in range(level_no + 2)])
            sib_row = wide([taken[bit][base + col] for col in range(level_no + 2)])
            is_left = side(bit) == 0
            left_row = jnp.where(is_left, own_row, sib_row)
            right_row = jnp.where(is_left, sib_row, own_row)
            state = []

            def inverse_of(matrix):
                inverse, power = fixed_inverse(matrix)
                state.append(jnp.max((power * power).reshape(rank // 8, 8, rank), axis=0))
                return inverse

            coef_a, coef_b = solve_pair(left_row, right_row, inverse_of)
            flag = jnp.maximum(flag, state[0])
            own_coef = jnp.where(is_left, coef_a, coef_b)
            for col in range(level_no + 1):
                coef[coef_slot(level_no, col)] = own_coef[:, col * rank : (col + 1) * rank]
            if level_no == 0:
                out_ref[...] = moved[:, :rank] - dot3(moved[:, rank:], own_coef)
            else:
                change_of = changes(coef_a, coef_b, left_row, right_row)
        if rest:
            following = level_no - 1 < levels
            late = rest[1:] if following else []
            late_change = change_of
            if late:
                settle(bit, rest[0])
                begin(bit, late[0])
            for row in rest[:1] if following else rest:
                merge_row(bit, row, change_of)
                begin(bit + 1, row)
        if bit:
            flag_copy.wait_recv()
            flag = jnp.maximum(flag, flag_in[bit])
    flag_ref[0, 0] = jnp.sum(flag)
    for copy in pending:
        copy.wait_send()


def fused(bases, targets, depth):
    levels, rows, rank = bases.shape
    stages = [
        pltpu.VMEM((offset(min(depth - bit, levels)), rank, rank), jnp.float32)
        for bit in range(depth)
    ]
    dma = pltpu.SemaphoreType.DMA
    return pl.pallas_call(
        functools.partial(fused_kernel, depth),
        out_shape=(
            jax.ShapeDtypeStruct(targets.shape, jnp.float32),
            jax.ShapeDtypeStruct((1, 1), jnp.float32),
        ),
        in_specs=[pl.BlockSpec(memory_space=pl.ANY)] * 2,
        out_specs=(VMEM_SPEC, pl.BlockSpec(memory_space=pltpu.SMEM)),
        scratch_shapes=stages
        + stages
        + [
            pltpu.VMEM((levels * (levels + 1) // 2, rank, rank), jnp.float32),
            pltpu.VMEM((rank, 2 * rank), jnp.float32),
            pltpu.VMEM((rows, 2 * rank), jnp.float32),
            pltpu.VMEM((depth, 8, 128), jnp.float32),
            pltpu.VMEM((depth, 8, 128), jnp.float32),
            pltpu.VMEM(bases.shape, jnp.float32),
            pltpu.VMEM(targets.shape, jnp.float32),
            dma((levels + 1,)),
        ]
        + [dma((depth, levels))] * 2
        + [dma((depth,))] * 6,
        compiler_params=pltpu.CompilerParams(
            collective_id=0, has_side_effects=True, vmem_limit_bytes=FUSED_LIMIT
        ),
    )(bases, targets)


def general(bases, targets):
    levels, _, rank = bases.shape
    tree_depth = lax.axis_size(AXIS).bit_length() - 1
    sums = call(gram_kernel, blocks(offset(levels), rank), (bases, targets))
    for bit_no in range(tree_depth - levels):
        sums = sums + from_partner(sums, bit_no)
    coefs = [None] * levels
    for level_no in reversed(range(levels)):
        group_bits = tree_depth - level_no - 1
        sibling = from_partner(sums, group_bits)
        outs = [blocks(level_no + 1, rank)]
        if level_no:
            outs.append(blocks(offset(level_no), rank))
        kernel = functools.partial(level_kernel, level_no, group_bits)
        coefs[level_no], *rest = call(kernel, tuple(outs), (sums, sibling))
        sums = rest[0] if rest else None
    out = jax.ShapeDtypeStruct(targets.shape, jnp.float32)
    return call(apply_kernel, out, (bases, targets, *coefs))


def per_device(bases, targets):
    depth = lax.axis_size(AXIS).bit_length() - 1
    out, residual = fused(bases, targets, depth)
    limit = (RESIDUAL / bases.shape[2]) ** 2
    return lax.cond(
        residual[0, 0] < limit, lambda b, t, o: o, lambda b, t, o: general(b, t), bases, targets, out
    )


def solution(mesh):
    return jax.shard_map(
        per_device,
        mesh=mesh,
        in_specs=(P(None, AXIS, None), P(AXIS, None)),
        out_specs=P(AXIS, None),
        check_vma=False,
    )
```

```python
import functools

import jax
import jax.numpy as jnp
from jax import lax
from jax.experimental import pallas as pl
from jax.experimental.pallas import tpu as pltpu
from jax.sharding import PartitionSpec as P

AXIS = "rows"
VMEM_LIMIT = 48 * 2**20
FUSED_LIMIT = 62 * 2**20
VMEM_SPEC = pl.BlockSpec(memory_space=pltpu.VMEM)


def offset(level_no):
    return level_no * (level_no + 3) // 2


def split(value):
    high = value.astype(jnp.bfloat16)
    low = (value - high.astype(jnp.float32)).astype(jnp.bfloat16)
    return high, low


def dot_split(left, right):
    left_high, left_low = left
    right_high, right_low = right
    dot = functools.partial(jnp.dot, preferred_element_type=jnp.float32)
    return (dot(left_low, right_high) + dot(left_high, right_low)) + dot(left_high, right_high)


def dot3(left, right):
    return dot_split(split(left), split(right))


def wide(blocks):
    return jnp.concatenate(blocks, axis=1)


def gram_rows(bases_ref, targets_ref, store):
    levels = bases_ref.shape[0]
    rank = bases_ref.shape[2]
    parts = [split(targets_ref[...])]
    for level_no in range(levels):
        basis = bases_ref[level_no]
        parts.append(split(basis))
        turned = split(basis.T)
        rhs = (wide([part[0] for part in parts]), wide([part[1] for part in parts]))
        row = dot_split(turned, rhs)
        for col in range(level_no + 2):
            store(offset(level_no) + col, row[:, col * rank : (col + 1) * rank])


def eye(rank):
    shape = (rank, rank)
    row = lax.broadcasted_iota(jnp.int32, shape, 0)
    col = lax.broadcasted_iota(jnp.int32, shape, 1)
    return (row == col).astype(jnp.float32)


def square_step(inverse, power):
    rank = power.shape[0]
    both = dot3(power, wide([inverse, power]))
    return inverse + both[:, :rank], both[:, rank:]


def solve_pair(left_row, right_row, inverse_of):
    rank = left_row.shape[0]
    gram_a, gram_b = left_row[:, -rank:], right_row[:, -rank:]
    proj_a, proj_b = left_row[:, :-rank], right_row[:, :-rank]
    first = dot3(gram_a, wide([gram_b, proj_b]))
    inverse = inverse_of(first[:, :rank])
    coef_b = dot3(inverse, proj_a - first[:, rank:])
    coef_a = proj_b - dot3(gram_b, coef_b)
    return coef_a, coef_b


def adaptive_inverse(matrix):
    identity = eye(matrix.shape[0])

    def unfinished(state):
        step, _, power = state
        size = jnp.sum(power * power)
        return jnp.logical_and(size > 1e-14, step < 64)

    def body(state):
        step, inverse, power = state
        inverse, power = square_step(inverse, power)
        return step + 1, inverse, power

    state = (0, identity + matrix, dot3(matrix, matrix))
    return lax.while_loop(unfinished, body, state)[1]


def merged_rows(level_no, own, sib, sides, coef_a, coef_b, store):
    rank = coef_a.shape[0]
    proj_a, proj_b = sides[0][:, :-rank], sides[1][:, :-rank]
    stacked = jnp.concatenate([coef_a, coef_b], axis=0)
    rhs = split(jnp.concatenate([proj_a + coef_b, proj_b + coef_a], axis=0))
    for row_no in range(level_no):
        columns = slice((row_no + 1) * rank, (row_no + 2) * rank)
        turned = split(stacked[:, columns].T)
        end = (row_no + 2) * rank
        change = dot_split(turned, (rhs[0][:, :end], rhs[1][:, :end]))
        for col in range(row_no + 2):
            slot = offset(row_no) + col
            store(slot, own(slot) + sib(slot) - change[:, col * rank : (col + 1) * rank])


def final_coefs(coef_of, levels):
    deltas = []
    for level_no in range(levels):
        delta = coef_of(level_no, 0)
        if deltas:
            known = jnp.concatenate(deltas, axis=0)
            delta = delta - dot3(wide([coef_of(level_no, 1 + i) for i in range(level_no)]), known)
        deltas.append(delta)
    return deltas


def gram_kernel(bases_ref, targets_ref, out_ref):
    def store(slot, value):
        out_ref[slot] = value

    gram_rows(bases_ref, targets_ref, store)


def level_kernel(level_no, group_bits, own_ref, sib_ref, *out_refs):
    coef_ref = out_refs[0]
    is_left = lax.rem(lax.axis_index(AXIS) // 2**group_bits, 2) == 0
    base = offset(level_no)
    own_row = wide([own_ref[base + col] for col in range(level_no + 2)])
    sib_row = wide([sib_ref[base + col] for col in range(level_no + 2)])
    sides = (jnp.where(is_left, own_row, sib_row), jnp.where(is_left, sib_row, own_row))
    coef_a, coef_b = solve_pair(*sides, adaptive_inverse)
    own_coef = jnp.where(is_left, coef_a, coef_b)
    rank = coef_a.shape[0]
    for col in range(level_no + 1):
        coef_ref[col] = own_coef[:, col * rank : (col + 1) * rank]
    if level_no:
        next_ref = out_refs[1]

        def store(slot, value):
            next_ref[slot] = value

        merged_rows(
            level_no, lambda s: own_ref[s], lambda s: sib_ref[s], sides, coef_a, coef_b, store
        )


def apply_kernel(bases_ref, targets_ref, *refs):
    levels = bases_ref.shape[0]
    coefs, out_ref = refs[:-1], refs[-1]
    deltas = final_coefs(lambda level_no, col: coefs[level_no][col], levels)
    lhs = wide([bases_ref[level_no] for level_no in range(levels)])
    out_ref[...] = targets_ref[...] - dot3(lhs, jnp.concatenate(deltas, axis=0))


def call(kernel, outs, args):
    return pl.pallas_call(
        kernel,
        out_shape=outs,
        in_specs=[VMEM_SPEC] * len(args),
        out_specs=jax.tree.map(lambda _: VMEM_SPEC, outs),
        compiler_params=pltpu.CompilerParams(vmem_limit_bytes=VMEM_LIMIT),
    )(*args)


def from_partner(value, bit_no):
    pairs = [(source, source ^ 2**bit_no) for source in range(lax.axis_size(AXIS))]
    return lax.ppermute(value, AXIS, pairs)


def blocks(count, rank):
    return jax.ShapeDtypeStruct((count, rank, rank), jnp.float32)


SQUARINGS = 3
RESIDUAL = 1e-7


def fixed_inverse(matrix):
    inverse, power = eye(matrix.shape[0]) + matrix, dot3(matrix, matrix)
    for _ in range(SQUARINGS):
        inverse, power = square_step(inverse, power)
    return inverse, power


def fused_kernel(depth, bases_in, targets_in, out_ref, flag_ref, *refs):
    levels, _, rank = bases_in.shape
    half = rank // 2
    sums, taken = refs[:depth], refs[depth : 2 * depth]
    coef, turned_ref, moved, flag_own, flag_in = refs[2 * depth : 2 * depth + 5]
    bases_ref, targets_ref, load = refs[2 * depth + 5 : 2 * depth + 8]
    sems = refs[2 * depth + 8 :]
    loads = [pltpu.make_async_copy(targets_in, targets_ref, load.at[levels])]
    for level_no in range(levels):
        loads.append(
            pltpu.make_async_copy(
                bases_in.at[level_no], bases_ref.at[level_no], load.at[level_no]
            )
        )
    for copy in loads:
        copy.start()
    link_send, link_recv, core_send, core_recv, relay_send, relay_recv, flag_send, flag_recv = sems
    me = lax.axis_index(AXIS)
    core = lax.rem(me, 2)
    own_half = pl.ds(pl.multiple_of(core * half, half), half)
    other_half = pl.ds(pl.multiple_of((1 - core) * half, half), half)
    pending = []

    def side(bit):
        return lax.rem(me // 2**bit, 2)

    def partner(bit):
        return me + 2**bit * (1 - 2 * side(bit))

    def push(src, dst, send, recv, bit):
        copy = pltpu.make_async_remote_copy(
            src_ref=src,
            dst_ref=dst,
            send_sem=send,
            recv_sem=recv,
            device_id=(partner(bit),),
            device_id_type=pl.DeviceIdType.MESH,
        )
        copy.start()
        pending.append(copy)
        return copy

    barrier = pltpu.get_barrier_semaphore()
    for bit in range(depth):
        pl.semaphore_signal(
            barrier, inc=1, device_id=(partner(bit),), device_id_type=pl.DeviceIdType.MESH
        )

    links, swaps = {}, {}

    def send_row(bit, row):
        slots = pl.ds(offset(row), row + 2)
        critical = row == depth - 1 - bit
        if bit == 0:
            region = (slots,) if critical else (slots, other_half)
        else:
            region = (slots, own_half)
        src, dst = sums[bit].at[region], taken[bit].at[region]
        links[bit, row] = push(src, dst, link_send.at[bit, row], link_recv.at[bit, row], bit)
        if critical and bit:
            swaps[bit] = push(src, src, core_send.at[bit], core_recv.at[bit], 0)

    def begin(bit, row):
        if (bit, row) not in links:
            send_row(bit, row)

    def settle(bit, row):
        copy = links[bit, row]
        if bit and any(copy is other for other in pending):
            copy.wait_send()
            pending[:] = [other for other in pending if other is not copy]

    parts = []
    for place, copy in enumerate(loads):
        copy.wait()
        parts.append(split(bases_ref[place - 1] if place else targets_ref[...]))
    high, low = wide([part[0] for part in parts]), wide([part[1] for part in parts])
    for row in reversed(range(levels)):
        end = (row + 2) * rank
        value = dot_split(split(bases_ref[row].T), (high[:, :end], low[:, :end]))
        for col in range(row + 2):
            sums[0][offset(row) + col] = value[:, col * rank : (col + 1) * rank]
        if row == levels - 1:
            pl.semaphore_wait(barrier, depth)
        send_row(0, row)

    def coef_slot(level_no, col):
        return level_no * (level_no + 1) // 2 + col

    def move_rows():
        deltas = []
        for level_no in range(1, levels):
            delta = wide([coef[coef_slot(level_no, col)] for col in range(2)])
            if deltas:
                lhs = wide([coef[coef_slot(level_no, 1 + i)] for i in range(1, level_no)])
                delta = delta - dot3(lhs, jnp.concatenate(deltas, axis=0))
            deltas.append(delta)
        change = dot_split((high[:, 2 * rank :], low[:, 2 * rank :]), split(jnp.concatenate(deltas, axis=0)))
        moved[:, :rank] = targets_ref[...] - change[:, :rank]
        moved[:, rank:] = bases_ref[0] - change[:, rank:]

    def merge_row(bit, row, change_of):
        links[bit, row].wait_recv()
        change = change_of(row)
        for col in range(row + 2):
            slot = offset(row) + col
            value = sums[bit][slot, own_half, :] + taken[bit][slot, own_half, :]
            if change is not None:
                value = value - change[:, col * rank : (col + 1) * rank]
            sums[bit + 1][slot, own_half, :] = value

    def changes(coef_a, coef_b, left_row, right_row):
        proj_a, proj_b = left_row[:, :-rank], right_row[:, :-rank]
        stacked = jnp.concatenate([coef_a, coef_b], axis=0)
        rhs = split(jnp.concatenate([proj_a + coef_b, proj_b + coef_a], axis=0))

        def change_of(row):
            turned_ref[...] = stacked[:, (row + 1) * rank : (row + 2) * rank].T
            end = (row + 2) * rank
            return dot_split(split(turned_ref[own_half, :]), (rhs[0][:, :end], rhs[1][:, :end]))

        return change_of

    flag = jnp.zeros((8, 128), jnp.float32)
    late, late_change = [], None
    for bit in range(depth):
        level_no = depth - 1 - bit
        solving = level_no < levels
        rest = list(reversed(range(min(level_no, levels))))
        if bit:
            flag_own[bit] = flag
            flag_copy = push(
                flag_own.at[bit], flag_in.at[bit], flag_send.at[bit], flag_recv.at[bit], bit
            )
        if level_no == 0:
            move_rows()
        change_of = lambda row: None
        if solving:
            for place, row in enumerate(late):
                settle(bit - 1, row)
                if place + 1 < len(late):
                    begin(bit - 1, late[place + 1])
                merge_row(bit - 1, row, late_change)
            slots = pl.ds(offset(level_no), level_no + 2)
            links[bit, level_no].wait_recv()
            if bit:
                region = taken[bit].at[slots, own_half]
                relay = push(region, region, relay_send.at[bit], relay_recv.at[bit], 0)
            if rest:
                begin(bit, rest[0])
            if bit:
                swaps[bit].wait_recv()
                relay.wait_recv()
            base = offset(level_no)
            own_row = wide([sums[bit][base + col] for col in range(level_no + 2)])
            sib_row = wide([taken[bit][base + col] for col in range(level_no + 2)])
            is_left = side(bit) == 0
            left_row = jnp.where(is_left, own_row, sib_row)
            right_row = jnp.where(is_left, sib_row, own_row)
            state = []

            def inverse_of(matrix):
                inverse, power = fixed_inverse(matrix)
                state.append(jnp.max((power * power).reshape(rank // 8, 8, rank), axis=0))
                return inverse

            coef_a, coef_b = solve_pair(left_row, right_row, inverse_of)
            flag = jnp.maximum(flag, state[0])
            own_coef = jnp.where(is_left, coef_a, coef_b)
            for col in range(level_no + 1):
                coef[coef_slot(level_no, col)] = own_coef[:, col * rank : (col + 1) * rank]
            if level_no == 0:
                out_ref[...] = moved[:, :rank] - dot3(moved[:, rank:], own_coef)
            else:
                change_of = changes(coef_a, coef_b, left_row, right_row)
        if rest:
            following = level_no - 1 < levels
            late = rest[1:] if following else []
            late_change = change_of
            if late:
                settle(bit, rest[0])
                begin(bit, late[0])
            for row in rest[:1] if following else rest:
                merge_row(bit, row, change_of)
                begin(bit + 1, row)
        if bit:
            flag_copy.wait_recv()
            flag = jnp.maximum(flag, flag_in[bit])
    flag_ref[0, 0] = jnp.sum(flag)
    for copy in pending:
        copy.wait_send()


def fused(bases, targets, depth):
    levels, rows, rank = bases.shape
    stages = [
        pltpu.VMEM((offset(min(depth - bit, levels)), rank, rank), jnp.float32)
        for bit in range(depth)
    ]
    dma = pltpu.SemaphoreType.DMA
    return pl.pallas_call(
        functools.partial(fused_kernel, depth),
        out_shape=(
            jax.ShapeDtypeStruct(targets.shape, jnp.float32),
            jax.ShapeDtypeStruct((1, 1), jnp.float32),
        ),
        in_specs=[pl.BlockSpec(memory_space=pl.ANY)] * 2,
        out_specs=(VMEM_SPEC, pl.BlockSpec(memory_space=pltpu.SMEM)),
        scratch_shapes=stages
        + stages
        + [
            pltpu.VMEM((levels * (levels + 1) // 2, rank, rank), jnp.float32),
            pltpu.VMEM((rank, 2 * rank), jnp.float32),
            pltpu.VMEM((rows, 2 * rank), jnp.float32),
            pltpu.VMEM((depth, 8, 128), jnp.float32),
            pltpu.VMEM((depth, 8, 128), jnp.float32),
            pltpu.VMEM(bases.shape, jnp.float32),
            pltpu.VMEM(targets.shape, jnp.float32),
            dma((levels + 1,)),
        ]
        + [dma((depth, levels))] * 2
        + [dma((depth,))] * 6,
        compiler_params=pltpu.CompilerParams(
            collective_id=0, has_side_effects=True, vmem_limit_bytes=FUSED_LIMIT
        ),
    )(bases, targets)


def general(bases, targets):
    levels, _, rank = bases.shape
    tree_depth = lax.axis_size(AXIS).bit_length() - 1
    sums = call(gram_kernel, blocks(offset(levels), rank), (bases, targets))
    for bit_no in range(tree_depth - levels):
        sums = sums + from_partner(sums, bit_no)
    coefs = [None] * levels
    for level_no in reversed(range(levels)):
        group_bits = tree_depth - level_no - 1
        sibling = from_partner(sums, group_bits)
        outs = [blocks(level_no + 1, rank)]
        if level_no:
            outs.append(blocks(offset(level_no), rank))
        kernel = functools.partial(level_kernel, level_no, group_bits)
        coefs[level_no], *rest = call(kernel, tuple(outs), (sums, sibling))
        sums = rest[0] if rest else None
    out = jax.ShapeDtypeStruct(targets.shape, jnp.float32)
    return call(apply_kernel, out, (bases, targets, *coefs))


def per_device(bases, targets):
    depth = lax.axis_size(AXIS).bit_length() - 1
    out, residual = fused(bases, targets, depth)
    limit = (RESIDUAL / bases.shape[2]) ** 2
    return lax.cond(
        residual[0, 0] < limit, lambda b, t, o: o, lambda b, t, o: general(b, t), bases, targets, out
    )


def solution(mesh):
    return jax.shard_map(
        per_device,
        mesh=mesh,
        in_specs=(P(None, AXIS, None), P(AXIS, None)),
        out_specs=P(AXIS, None),
        check_vma=False,
    )
```
